256 devices in a mesh: grp: 8 (over y, core), seg: 32 (over z, x).
Axes of the slice: x: 4, y: 4, z: 8, core: 2. Of those that a mesh axis runs over, the one named last changes fastest.
Arguments:
- queries: bfloat16 [8, 128, 8192], P('grp', 'seg'), may hold values from -96 to 96
- keys: bfloat16 [8, 4096, 1024], P('grp', 'seg'), may hold values from -6 to 6
- values: bfloat16 [8, 4096, 1024], P('grp', 'seg'), may hold values from -6 to 6
- node_ids: int32 [8, 4096], P('grp'), may hold values from 0 to 127, never falling along the last dimension, each value on 1 to 96 neighbouring positions
- parents: int32 [8, 128], P('grp'), may hold values from 0 to 126, as said below
- score_pos: int32 [8, 128], P('grp'), may hold values from 0 to 4095, as said below
- out_weight: bfloat16 [8192, 5120], P('seg'), may hold values from -0.0625 to 0.0625
- resid: bfloat16 [8, 128, 5120], P('grp', 'seg'), may hold values from -6 to 6
- norm_gain: bfloat16 [5120], replicated, may hold values from 0.5 to 1.5
- vocab_weight: bfloat16 [5120, 98304], P(None, ('grp', 'seg')), may hold values from -8 to 8
- targets: int32 [8, 128], P('grp', 'seg'), may hold values from 0 to 98303
- old_logp: float32 [8, 128], P('grp', 'seg'), may hold values from -18.5 to -13.5
- leaf_node: int32 [8, 64], P('grp'), may hold values from 0 to 127
- advantages: float32 [8, 64], P('grp', 'seg'), may hold values from -4 to 4
Outputs:
- token_logratio: float32 [8, 128], P('grp', 'seg')
- leaf_logratio: float32 [8, 64], P('grp', 'seg')
- loss: float32 [], replicated
The draws below stay inside these ranges and needn't reach their ends.
Inputs may be any that keep to these rules, and one draw needn't show every extreme that they name: `parents`: node n's parent is n when n is a multiple of 8, the root of a tree of 8 consecutive nodes; otherwise an earlier node of the same tree, and the last node of each tree has the node before it as parent. `score_pos`: scored row r lies in packed positions (r // 4) * 128 to (r // 4 + 1) * 128 - 1; a group's first scored row is at position 0 and its last at 4095.
All inputs are finite; a program needn't handle non-finite values.
Results may differ from the reference program's by a relative error of at most 0.0095.
Values may be sent and summed in bfloat16 or wider, within the bound.
A program may use at most 128 MiB of HBM per device.

```python
import math
import jax
import jax.numpy as jnp
import numpy as np
from jax import lax

D = 5120
QUERY_HEADS = 64
KEY_VALUE_HEADS = 8
HEAD_SIZE = 128
VOC_DEV = 384
TOK_DEV = 128
SCORE_DEV = 4
NPT = 8
TREE_GROUPS = 8
GROUP_TOKENS = 4096
SCORED_POSITIONS = 128
NODES = 128
LEAVES = 64
SEG_MOST = 96
VOCAB = 98304


def score_rows(key):
    key = jax.random.fold_in(key, 101)
    row_index = jnp.arange(SCORED_POSITIONS, dtype=jnp.int32)
    offsets = jax.random.randint(key, (TREE_GROUPS, SCORED_POSITIONS), 0, TOK_DEV, dtype=jnp.int32)
    offsets = jnp.where((row_index == 0)[None, :], 0, offsets)
    offsets = jnp.where((row_index == SCORED_POSITIONS - 1)[None, :], TOK_DEV - 1, offsets)
    return (row_index // SCORE_DEV)[None, :] * TOK_DEV + offsets


def key_field(key):
    key = jax.random.fold_in(key, 202)
    return jnp.clip(jax.random.normal(key, (TREE_GROUPS, GROUP_TOKENS, KEY_VALUE_HEADS * HEAD_SIZE), jnp.float32), -6.0, 6.0)


def slot_layout():
    row_blocks = (SCORED_POSITIONS + 15) // 16
    slot_count = TREE_GROUPS * row_blocks
    block_width = VOCAB // slot_count
    return (row_blocks, block_width, block_width // 3)


def target_ids(key):
    key = jax.random.fold_in(key, 303)
    row_blocks, block_width, third = slot_layout()
    upper = jax.random.randint(jax.random.fold_in(key, 1), (TREE_GROUPS, SCORED_POSITIONS), 1, VOCAB + 1, dtype=jnp.int32)
    spread = jax.random.randint(jax.random.fold_in(key, 2), (TREE_GROUPS, SCORED_POSITIONS), 0, upper, dtype=jnp.int32)
    row_index = jnp.arange(SCORED_POSITIONS, dtype=jnp.int32)
    group_index = jnp.arange(TREE_GROUPS, dtype=jnp.int32)
    slot = group_index[:, None] * row_blocks + (row_index // 16)[None, :]
    offset = jax.random.randint(jax.random.fold_in(key, 3), (TREE_GROUPS, SCORED_POSITIONS), 0, third, dtype=jnp.int32)
    aligned = (row_index % 16 == 0)[None, :]
    return jnp.where(aligned, slot * block_width + offset, spread)


def draw_score_pos(key, part):
    return score_rows(key)


def draw_keys(key, part):
    return key_field(key).astype(jnp.bfloat16)


def draw_targets(key, part):
    return target_ids(key)


def draw_queries(key, part):
    key = jax.random.fold_in(key, 3)
    base = jax.random.normal(key, (TREE_GROUPS, SCORED_POSITIONS, QUERY_HEADS * HEAD_SIZE), jnp.float32)
    return jnp.clip(base, -96.0, 96.0).astype(jnp.bfloat16)


def draw_resid(key, part):
    own_key = jax.random.fold_in(key, 11)
    base = jax.random.normal(own_key, (TREE_GROUPS, SCORED_POSITIONS, D), jnp.float32)
    return jnp.clip(0.25 * base, -1.5, 1.5).astype(jnp.bfloat16)


def draw_vocab_weight(key, part):
    own_key = jax.random.fold_in(key, 13)
    spread = (D // 9) ** (-0.5)
    base = jax.random.normal(own_key, (D, VOCAB), jnp.float32)
    return jnp.clip(spread * base, -6.0 * spread, 6.0 * spread).astype(jnp.bfloat16)


def draw_parents(key, part):
    key = jax.random.fold_in(key, 5)
    node_index = jnp.arange(NODES, dtype=jnp.int32)
    within = node_index % NPT
    picks = jax.random.randint(key, (TREE_GROUPS, NODES), 0, jnp.maximum(within, 1)[None, :], dtype=jnp.int32)
    picks = jnp.where((within == NPT - 1)[None, :], within[None, :] - 1, picks)
    return (node_index - within)[None, :] + picks


def place_ends(result, key, least, largest):
    longest = result.shape.index(max(result.shape))
    spots = []
    for shift in (0, 1):
        where = [jax.random.randint(jax.random.fold_in(key, axis), (), 0, length) for axis, length in enumerate(result.shape)]
        where[longest] = (where[longest] + shift) % result.shape[longest]
        spots.append(tuple(where))
    return result.at[spots[0]].set(least).at[spots[1]].set(largest)


def levels(key, dims, cuts, least, high):
    def one(axis_at, shards_of):
        steps = jax.random.uniform(jax.random.fold_in(jax.random.fold_in(key, 6), axis_at), (shards_of,), jnp.float32, least / len(cuts), high / len(cuts))
        return jnp.repeat(jnp.exp(steps), dims[axis_at] // shards_of).reshape((-1,) + (1,) * (len(dims) - axis_at - 1))

    level = one(*cuts[0])
    for cut in cuts[1:]:
        level = level * one(*cut)
    return level


def length_profile(count, total, bound, skew):
    loads = [(1 << 20) // math.isqrt(grade ** skew) + 1 for grade in range(2, count + 1)]
    rest, given = total - bound - (count - 1), [1] * (count - 1)
    while rest > 0:
        movable = [i for i in range(count - 1) if given[i] < bound]
        whole, remaining = sum([loads[i] for i in movable]), rest
        for i in movable:
            more = min(bound - given[i], max(1, remaining * loads[i] // whole), rest)
            given[i] = given[i] + more
            rest = rest - more
    return np.array([bound] + given)


def uneven(rng, number_of, total, most, slope):
    if number_of == 2:
        one = jax.random.randint(rng, (), max(1, total - most), min(most, total - 1) + 1)
        return jnp.stack([one, total - one])
    lengths = jnp.asarray(length_profile(number_of, total, most, slope), jnp.int32)
    twos = (number_of - 1) // 2
    donor, taker = lengths[1:1 + 2 * twos:2], lengths[2:2 + 2 * twos:2]
    slack = jnp.minimum(donor - 1, most - taker)
    shifted = jax.random.randint(jax.random.fold_in(rng, 1), (twos,), 0, 1 << 20) % (slack + 1)
    lengths = lengths.at[1:1 + 2 * twos:2].set(donor - shifted).at[2:2 + 2 * twos:2].set(taker + shifted)
    return lengths[jax.random.permutation(jax.random.fold_in(rng, 2), number_of)]


def centred(key, dims, width, most, pieces=(), kind=jnp.bfloat16):
    drawn = width * jax.random.normal(key, dims, jnp.float32)
    if pieces:
        drawn = drawn * levels(key, dims, pieces, -0.22, 0.18)
    return jnp.clip(drawn, -most, most).astype(kind)


def setup_inputs(seed: int = 0) -> dict:
    key_of = jax.random.split(jax.random.key(seed), 15)
    return {
        "queries": draw_queries(jax.random.fold_in(key_of[14], 71), 0),
        "keys": draw_keys(jax.random.fold_in(key_of[14], 71), 0),
        "values": centred(key_of[2], (TREE_GROUPS, GROUP_TOKENS, KEY_VALUE_HEADS * HEAD_SIZE), 1.0, 6.0, ((0, 8), (1, 32))),
        "node_ids": jax.vmap(lambda own: jnp.searchsorted(jnp.cumsum(uneven(own, NODES, GROUP_TOKENS, SEG_MOST, 2)), jnp.arange(GROUP_TOKENS), side="right"))(jax.random.split(key_of[3], TREE_GROUPS)).reshape((TREE_GROUPS, GROUP_TOKENS)).astype(jnp.int32),
        "parents": draw_parents(jax.random.fold_in(key_of[14], 71), 0),
        "score_pos": draw_score_pos(jax.random.fold_in(key_of[14], 71), 0),
        "out_weight": centred(key_of[6], (QUERY_HEADS * HEAD_SIZE, D), (QUERY_HEADS * HEAD_SIZE) ** -0.5, 0.0625, ((0, 32),)),
        "resid": draw_resid(jax.random.fold_in(key_of[14], 71), 0),
        "norm_gain": jnp.clip(1.0 + 0.1 * jax.random.normal(key_of[8], (D,), jnp.float32), 0.5, 1.5).astype(jnp.bfloat16),
        "vocab_weight": draw_vocab_weight(jax.random.fold_in(key_of[14], 71), 0),
        "targets": draw_targets(jax.random.fold_in(key_of[14], 71), 0),
        "old_logp": jnp.clip(-18.5 + 5.0 * jax.random.uniform(key_of[11], (TREE_GROUPS, SCORED_POSITIONS), jnp.float32) ** levels(key_of[11], (TREE_GROUPS, SCORED_POSITIONS), ((0, 8), (1, 32)), -0.2, 0.2), -18.5, -13.5),
        "leaf_node": place_ends(jax.random.randint(key_of[12], (TREE_GROUPS, LEAVES), 0, NODES), jax.random.fold_in(key_of[12], 1), 0, NODES - 1).astype(jnp.int32),
        "advantages": centred(key_of[13], (TREE_GROUPS, LEAVES), 1.0, 4.0, ((0, 8), (1, 32)), jnp.float32),
    }


HIGH = lax.Precision.HIGHEST
EPS_LOW = 0.0003
EPS_HIGH = 0.0004
NEGATIVE = -1e+30

def ancestors(parent_list):
    node_count = parent_list.shape[0]
    node_index = jnp.arange(node_count, dtype=jnp.int32)
    parent_hot = (parent_list[:, None] == node_index[None, :]).astype(jnp.float32)
    identity = (node_index[:, None] == node_index[None, :]).astype(jnp.float32)
    closure = jnp.minimum(identity + parent_hot, 1.0)
    for squaring in range(max(1, (node_count - 1).bit_length())):
        closure = jnp.minimum(jnp.dot(closure, closure, precision=HIGH), 1.0)
    return closure

def node_hot(node_list, node_count):
    node_index = jnp.arange(node_count, dtype=jnp.int32)
    return (node_list[:, None] == node_index[None, :]).astype(jnp.float32)

def rms_normalize(hidden, norm_gain):
    power = lax.optimization_barrier(jnp.mean(hidden * hidden, axis=-1, keepdims=True))
    return (hidden * lax.rsqrt(power + 1e-06) * norm_gain.astype(jnp.float32)).astype(jnp.bfloat16)

def attend(query_matrix, key_matrix, value_matrix, visible):
    count_of_rows = query_matrix.shape[0]
    per_head_queries = query_matrix.reshape(count_of_rows, KEY_VALUE_HEADS, QUERY_HEADS // KEY_VALUE_HEADS, HEAD_SIZE).astype(jnp.float32)
    per_head_keys = key_matrix.reshape(-1, KEY_VALUE_HEADS, HEAD_SIZE).astype(jnp.float32)
    per_head_values = value_matrix.reshape(-1, KEY_VALUE_HEADS, HEAD_SIZE).astype(jnp.float32)
    scores = jnp.einsum('rkgd,tkd->kgrt', per_head_queries, per_head_keys) * HEAD_SIZE ** (-0.5)
    scores = jnp.where(visible[None, None], scores, NEGATIVE)
    top = lax.optimization_barrier(jnp.max(scores, axis=-1, keepdims=True))
    raised = jnp.exp(scores - top)
    probs = (raised / lax.optimization_barrier(jnp.sum(raised, axis=-1, keepdims=True))).astype(jnp.bfloat16)
    mixed = jnp.einsum('kgrt,tkd->rkgd', probs.astype(jnp.float32), per_head_values)
    return mixed.astype(jnp.bfloat16).reshape(count_of_rows, QUERY_HEADS * HEAD_SIZE)

def reference(queries, keys, values, node_ids, parents, score_pos, out_weight, resid, norm_gain, vocab_weight, targets, old_logp, leaf_node, advantages):

    def one_group(items):
        query_matrix, key_matrix, value_matrix, node_row, parent_row, position_row, resid_rows = items
        closure = ancestors(parent_row)
        row_hot = node_hot(jnp.take(node_row, position_row), NODES)
        key_hot = node_hot(node_row, NODES)
        reach = jnp.dot(row_hot, closure, precision=HIGH)
        linked = lax.dot_general(reach, key_hot, (((1,), (1,)), ((), ())), precision=HIGH)
        token_index = jnp.arange(node_row.shape[0], dtype=jnp.int32)
        visible = (linked > 0.5) & (token_index[None, :] <= position_row[:, None])
        mixed = attend(query_matrix, key_matrix, value_matrix, visible)
        hidden = jnp.dot(mixed, out_weight, preferred_element_type=jnp.float32) + resid_rows.astype(jnp.float32)
        return rms_normalize(hidden, norm_gain)
    normed = lax.map(one_group, (queries, keys, values, node_ids, parents, score_pos, resid))
    rows_all = normed.reshape(-1, D)
    target_all = targets.reshape(-1)
    vocab_index = jnp.arange(VOC_DEV, dtype=jnp.int32)

    def vocab_step(carry, block_index):
        run_max, run_sum, run_target = carry
        base = (block_index * VOC_DEV).astype(jnp.int32)
        block = lax.dynamic_slice_in_dim(vocab_weight, base, VOC_DEV, 1)
        logits = jnp.dot(rows_all, block, preferred_element_type=jnp.float32)
        local_max = lax.optimization_barrier(jnp.max(logits, axis=1))
        local_sum = lax.optimization_barrier(jnp.sum(jnp.exp(logits - local_max[:, None]), axis=1))
        hit = vocab_index[None, :] == (target_all - base)[:, None]
        picked = lax.optimization_barrier(jnp.sum(jnp.where(hit, logits, 0.0), axis=1))
        joined = jnp.maximum(run_max, local_max)
        total = run_sum * jnp.exp(run_max - joined) + local_sum * jnp.exp(local_max - joined)
        return ((joined, total, run_target + picked), None)
    start = (jnp.full(target_all.shape, NEGATIVE, jnp.float32), jnp.zeros(target_all.shape, jnp.float32), jnp.zeros(target_all.shape, jnp.float32))
    block_ids = jnp.arange(VOCAB // VOC_DEV, dtype=jnp.int32)
    (row_max, row_sum, row_target), unused = lax.scan(vocab_step, start, block_ids)
    logp = row_target - row_max - jnp.log(row_sum)
    token_logratio = logp.reshape(targets.shape) - old_logp

    def leaf_group(parent_row, node_row, position_row, leaf_row, ratio_row):
        closure = ancestors(parent_row)
        row_hot = node_hot(jnp.take(node_row, position_row), NODES)
        leaf_reach = jnp.dot(node_hot(leaf_row, NODES), closure, precision=HIGH)
        path = lax.dot_general(leaf_reach, row_hot, (((1,), (1,)), ((), ())), precision=HIGH)
        sums = jnp.dot(path, ratio_row, precision=HIGH)
        counts = lax.optimization_barrier(jnp.sum(path, axis=1))
        return sums / jnp.maximum(counts, 1.0)
    leaf_logratio = jax.vmap(leaf_group)(parents, node_ids, score_pos, leaf_node, token_logratio)
    ratio = jnp.exp(leaf_logratio)
    terms = jnp.minimum(ratio * advantages, jnp.clip(ratio, 1.0 - EPS_LOW, 1.0 + EPS_HIGH) * advantages)
    loss = -jnp.sum(terms) / (TREE_GROUPS * LEAVES)
    return (token_logratio, leaf_logratio, loss)
```

```python
import jax
import jax.numpy as jnp
from jax import lax
from jax.experimental import pallas as pl
from jax.experimental.pallas import tpu as pltpu
from jax.sharding import PartitionSpec as P

F32 = jnp.float32
BF16 = jnp.bfloat16
EPS_LOW = 0.0003
EPS_HIGH = 0.0004
NEGATIVE = -1e30
HEAD = 128
KV_HEADS = 8
X, Y, Z = 4, 4, 8
SEG = X * Z
GRP = 2 * Y
TOK = 128
ROWS = 128
NODES = 128
LEAVES = 64
SCORE = 4
WINDOW = 7
SLOTS = 8
D = 5120
DX = D // X
VOC = 384
CHUNKS = 4
CROWS = ROWS // CHUNKS
PARTS = ((0, 512, "xyz"), (512, 384, "yzx"), (896, 384, "zxy"))
MIB = 1024 * 1024


def iota(shape, dim):
    return lax.broadcasted_iota(jnp.int32, shape, dim)


def hot(mask):
    return mask.astype(F32).astype(BF16)


def mm(a, b):
    return jnp.dot(a, b, preferred_element_type=F32)


def mm_nt(a, b):
    return lax.dot_general(a, b, (((1,), (1,)), ((), ())), preferred_element_type=F32)


def closure_transposed(parent_row):
    sub = iota((NODES, NODES), 0)
    lane = iota((NODES, NODES), 1)
    step = jnp.where((sub == parent_row) | (sub == lane), 1.0, 0.0)
    for squaring in range(3):
        half = step.astype(BF16)
        step = jnp.minimum(mm(half, half), 1.0)
    return step.astype(BF16)


def scored_nodes(node_table, position_row):
    table = jnp.concatenate([node_table.astype(F32), jnp.zeros((TOK - SEG, TOK), F32)], axis=0)
    across = table.T.astype(BF16)
    sub = iota((TOK, ROWS), 0)
    lane = iota((TOK, ROWS), 1)
    spread = mm(across, hot(sub == lane // SCORE))
    match = sub == position_row - TOK * (lane // SCORE)
    return jnp.sum(jnp.where(match, spread, 0.0), axis=0, keepdims=True)


def attend_body(
    q_ref, k_ref, v_ref, node_ref, par_ref, pos_ref, ow_hbm, resid_ref, gain_ref,
    normed_ref,
    ow, qbuf, raised, parts, osend, obuf, aug, xsend, xown, xrecv, zsend, zown, zrecv, sqs, sqr,
    ow_sem, q_ss, q_rs, p_ss, p_rs, o_ss, o_rs, x_ss, x_rs, z_ss, z_rs, s_ss, s_rs,
):
    me = lax.axis_index("seg")
    z = me // X
    x = lax.rem(me, X)

    def at_x(delta):
        return {"seg": z * X + lax.rem(x + delta, X)}

    def at_z(delta):
        return {"seg": lax.rem(z + delta, Z) * X + x}

    ow_copy = pltpu.make_async_copy(ow_hbm, ow, ow_sem)
    ow_copy.start()
    barrier = pltpu.get_barrier_semaphore()

    def greet(delta, carry):
        pl.semaphore_signal(barrier, 1, device_id={"seg": lax.rem(me + delta, SEG)})
        return carry

    lax.fori_loop(1, SEG, greet, 0)

    for pair in range(SEG // 2):
        pieces = [
            q_ref[:, HEAD * (4 * pair + piece) : HEAD * (4 * pair + piece + 1)].astype(F32)
            for piece in range(4)
        ]
        qbuf[0, 16 * pair : 16 * pair + 16, :] = jnp.concatenate(pieces, axis=0).astype(BF16)
    qbuf[WINDOW] = jnp.zeros((2 * ROWS, HEAD), BF16)
    pl.semaphore_wait(barrier, SEG - 1)

    q_copies = []
    for slot in range(1, WINDOW):
        copy = pltpu.make_async_remote_copy(
            src_ref=qbuf.at[0],
            dst_ref=qbuf.at[slot],
            send_sem=q_ss.at[slot],
            recv_sem=q_rs.at[slot],
            device_id={"seg": lax.rem(me - slot + SEG, SEG)},
        )
        copy.start()
        q_copies.append(copy)

    aug[...] = jnp.zeros_like(aug)
    aug[0:SCORE, :] = resid_ref[...]
    closure_t = closure_transposed(par_ref[...])
    position_row = pos_ref[...]
    node_row = scored_nodes(node_ref[...], position_row)
    sub = iota((NODES, ROWS), 0)
    reach_t = mm(closure_t, hot(sub.astype(F32) == node_row)).astype(BF16)
    own_nodes = node_ref[pl.ds(me, 1), :]
    token_hot = jnp.where(sub == own_nodes, 1.0, 0.0).T.astype(BF16)
    linked = mm(token_hot, reach_t)
    visible = hot((linked > 0.5) & (sub + TOK * me <= position_row))
    wide_sub = iota((ROWS, 2 * ROWS), 0)
    wide_lane = iota((ROWS, 2 * ROWS), 1)
    wanted = lax.rem(SCORE * (me + wide_lane // 32) + lax.rem(wide_lane, SCORE), ROWS)
    mask = mm(visible, hot((wide_sub == wanted) & (wide_lane < 32 * WINDOW))) > 0.5

    for copy in q_copies:
        copy.wait_recv()

    scale = HEAD ** (-0.5)
    for k in range(KV_HEADS):
        query = qbuf[:, 32 * k : 32 * k + 32, :].reshape(2 * ROWS, HEAD)
        lanes = slice(HEAD * k, HEAD * k + HEAD)
        scores = jnp.where(mask, mm_nt(k_ref[:, lanes], query) * scale, NEGATIVE)
        top = jnp.max(scores, axis=0, keepdims=True)
        power = jnp.where(mask, jnp.exp(scores - top), 0.0)
        raised[k] = power
        parts[WINDOW - 1, k : k + 1, :] = top
        parts[WINDOW - 1, 8 + k : 9 + k, :] = jnp.sum(power, axis=0, keepdims=True)

    p_copies = []
    for delta in range(1, WINDOW):
        for way in (delta, -delta):
            copy = pltpu.make_async_remote_copy(
                src_ref=parts.at[WINDOW - 1],
                dst_ref=parts.at[WINDOW - 1 - way],
                send_sem=p_ss.at[WINDOW - 1 - way],
                recv_sem=p_rs.at[WINDOW - 1 - way],
                device_id={"seg": lax.rem(me + way + SEG, SEG)},
            )
            copy.start()
            p_copies.append(copy)
    for copy in p_copies:
        copy.wait_recv()
    part_slot = iota((8, 2 * ROWS), 1) // 32
    tops = []
    totals = []
    for away in range(1 - WINDOW, WINDOW):
        top = parts[away + WINDOW - 1, 0:8, :]
        total = parts[away + WINDOW - 1, 8:16, :]
        if away != 0:
            shift = (32 * away) % (2 * ROWS)
            top = pltpu.roll(top, shift, 1)
            total = pltpu.roll(total, shift, 1)
        valid = (part_slot >= away) & (part_slot < away + WINDOW)
        tops.append(jnp.where(valid, top, NEGATIVE))
        totals.append(jnp.where(valid, total, 0.0))
    peak = tops[0]
    for top in tops[1:]:
        peak = jnp.maximum(peak, top)
    whole = totals[0] * jnp.exp(tops[0] - peak)
    for top, total in zip(tops[1:], totals[1:]):
        whole = whole + total * jnp.exp(top - peak)
    factor = jnp.exp(parts[WINDOW - 1, 0:8, :] - peak) / jnp.where(whole > 0.0, whole, 1.0)
    for k in range(KV_HEADS):
        lanes = slice(HEAD * k, HEAD * k + HEAD)
        probs = raised[k] * factor[k : k + 1, :]
        mixed = mm(probs.T.astype(BF16), v_ref[:, lanes]).reshape(SLOTS, 4, 8, HEAD)
        for pair in range(4):
            osend[4 * k + pair] = mixed[0:WINDOW, pair].reshape(8 * WINDOW, HEAD)

    def o_copy(delta):
        there = lax.rem(me + delta, SEG)
        return pltpu.make_async_remote_copy(
            src_ref=osend.at[there],
            dst_ref=obuf.at[me],
            send_sem=o_ss.at[delta],
            recv_sem=o_rs.at[me],
            device_id={"seg": there},
        )

    def o_start(delta, carry):
        o_copy(delta).start()
        return carry

    lax.fori_loop(1, SEG, o_start, 0)
    obuf[me] = osend[me]

    def o_wait(delta, carry):
        source = lax.rem(me + delta, SEG)
        pltpu.make_async_remote_copy(
            src_ref=osend.at[source],
            dst_ref=obuf.at[source],
            send_sem=o_ss.at[delta],
            recv_sem=o_rs.at[source],
            device_id={"seg": source},
        ).wait_recv()
        return carry

    lax.fori_loop(1, SEG, o_wait, 0)

    sums = [None] * SEG
    for source in range(SEG):
        block = obuf[source]
        for slot in range(min(WINDOW, SEG - source)):
            row = source + slot
            term = block[8 * slot : 8 * slot + 8]
            sums[row] = term if sums[row] is None else sums[row] + term
    stacked = jnp.concatenate(sums, axis=0).astype(BF16)
    out_row = iota((2 * ROWS, 2 * ROWS), 0)
    in_row = iota((2 * ROWS, 2 * ROWS), 1)
    packed = lax.rem(out_row, ROWS)
    from_row = 8 * (packed // SCORE) + SCORE * (out_row // ROWS) + lax.rem(packed, SCORE)
    sorted_rows = mm(hot(in_row == from_row), stacked).astype(BF16)
    left = jnp.concatenate([sorted_rows[0:ROWS], sorted_rows[ROWS : 2 * ROWS]], axis=1)
    pick_row = iota((ROWS, 16), 0)
    pick_col = iota((ROWS, 16), 1)
    own_rows = hot((pick_row == SCORE * me + pick_col) & (pick_col < SCORE))

    def x_copy(delta, chunk):
        rows = pl.ds(pl.multiple_of(CROWS * lax.rem(chunk + z // 2, CHUNKS), CROWS), CROWS)
        return pltpu.make_async_remote_copy(
            src_ref=xsend.at[delta - 1, rows],
            dst_ref=xrecv.at[delta - 1, rows],
            send_sem=x_ss.at[delta - 1, chunk],
            recv_sem=x_rs.at[delta - 1, chunk],
            device_id=at_x(delta),
        )

    ow_copy.wait()
    for delta in (1, 3, 2, 0):
        cols = pl.ds(pl.multiple_of(DX * lax.rem(x + delta, X), DX), DX)
        product = mm(left, ow[:, cols]) + mm(own_rows, aug[:, cols])
        if delta == 0:
            xown[...] = product
        else:
            xsend[delta - 1] = encode(product)
            for chunk in range(CHUNKS):
                x_copy(delta, chunk).start()

    def z_copy(target, index):
        delta = lax.rem(target - z + Z, Z)
        return pltpu.make_async_remote_copy(
            src_ref=zsend.at[target],
            dst_ref=zrecv.at[delta],
            send_sem=z_ss.at[index],
            recv_sem=z_rs.at[delta],
            device_id={"seg": target * X + x},
        )

    for chunk in range(CHUNKS):
        for delta in (1, 3, 2):
            x_copy(delta, chunk).wait_recv()
        place = lax.rem(chunk + z // 2, CHUNKS)
        rows = pl.ds(pl.multiple_of(CROWS * place, CROWS), CROWS)
        total = xown[rows, :]
        for delta in (1, 3, 2):
            total = total + decode(xrecv[delta - 1, rows, :])
        for half in range(2):
            target = 2 * place + half
            piece = total[16 * half : 16 * half + 16]
            zsend[target] = encode(piece)

            @pl.when(target == z)
            def _():
                zown[...] = piece

            @pl.when(target != z)
            def _():
                z_copy(target, 2 * chunk + half).start()

    hidden = zown[...]
    for delta in range(1, Z):
        pltpu.make_async_remote_copy(
            src_ref=zsend.at[0],
            dst_ref=zrecv.at[delta],
            send_sem=z_ss.at[0],
            recv_sem=z_rs.at[delta],
            device_id=at_z(delta),
        ).wait_recv()
        hidden = hidden + decode(zrecv[delta])
    squares = jnp.sum(hidden * hidden, axis=1, keepdims=True)
    sqs[...] = jnp.broadcast_to(squares, sqs.shape)

    def s_copy(delta):
        return pltpu.make_async_remote_copy(
            src_ref=sqs,
            dst_ref=sqr.at[delta - 1],
            send_sem=s_ss.at[delta - 1],
            recv_sem=s_rs.at[delta - 1],
            device_id=at_x(delta),
        )

    for delta in range(1, X):
        s_copy(delta).start()
    gain = gain_ref[:, pl.ds(pl.multiple_of(DX * x, DX), DX)].astype(F32)
    for delta in range(1, X):
        s_copy(delta).wait_recv()
    power = (sqs[...] + sqr[0] + sqr[1] + sqr[2])[:, 0:1] / D
    normed_ref[...] = (hidden * lax.rsqrt(power + 1e-06) * gain).astype(BF16)

    for copy in q_copies + p_copies:
        copy.wait_send()

    def o_drain(delta, carry):
        o_copy(delta).wait_send()
        return carry

    lax.fori_loop(1, SEG, o_drain, 0)
    for delta in (1, 3, 2):
        for chunk in range(CHUNKS):
            x_copy(delta, chunk).wait_send()
    for chunk in range(CHUNKS):
        for half in range(2):
            target = 2 * lax.rem(chunk + z // 2, CHUNKS) + half

            @pl.when(target != z)
            def _():
                z_copy(target, 2 * chunk + half).wait_send()

    for delta in range(1, X):
        s_copy(delta).wait_send()


def encode(value):
    most = jnp.maximum(jnp.max(jnp.abs(value), axis=1, keepdims=True), 1e-30)
    level = jnp.ceil(jnp.log2(most * (1.0 / 32000.0)))
    scaled = jnp.round(value * jnp.exp2(-level)).astype(jnp.int32)
    levels = jnp.broadcast_to(level.astype(jnp.int32), (value.shape[0], HEAD))
    return jnp.concatenate([scaled, levels], axis=1).astype(jnp.int16)


def decode(code):
    wide = code.astype(jnp.int32).astype(F32)
    return wide[:, 0:DX] * jnp.exp2(wide[:, DX : DX + 1])


def vmem():
    return pl.BlockSpec(memory_space=pltpu.VMEM)


def attend(queries, keys, values, node_table, parents, positions, out_weight, resid, gain):
    sems = pltpu.SemaphoreType.DMA
    return pl.pallas_call(
        attend_body,
        out_shape=jax.ShapeDtypeStruct((16, DX), BF16),
        in_specs=[vmem()] * 6 + [pl.BlockSpec(memory_space=pl.ANY)] + [vmem()] * 2,
        out_specs=vmem(),
        scratch_shapes=[
            pltpu.VMEM((2 * HEAD, D), BF16),
            pltpu.VMEM((SLOTS, 2 * ROWS, HEAD), BF16),
            pltpu.VMEM((KV_HEADS, TOK, 2 * ROWS), F32),
            pltpu.VMEM((2 * WINDOW - 1, 16, 2 * ROWS), F32),
            pltpu.VMEM((SEG, 8 * WINDOW, HEAD), F32),
            pltpu.VMEM((SEG, 8 * WINDOW, HEAD), F32),
            pltpu.VMEM((16, D), BF16),
            pltpu.VMEM((X - 1, ROWS, DX + HEAD), jnp.int16),
            pltpu.VMEM((ROWS, DX), F32),
            pltpu.VMEM((X - 1, ROWS, DX + HEAD), jnp.int16),
            pltpu.VMEM((Z, 16, DX + HEAD), jnp.int16),
            pltpu.VMEM((16, DX), F32),
            pltpu.VMEM((Z, 16, DX + HEAD), jnp.int16),
            pltpu.VMEM((16, HEAD), F32),
            pltpu.VMEM((X - 1, 16, HEAD), F32),
            sems,
            sems((WINDOW,)),
            sems((WINDOW,)),
            sems((2 * WINDOW - 1,)),
            sems((2 * WINDOW - 1,)),
            sems((SEG,)),
            sems((SEG,)),
            sems((X - 1, CHUNKS)),
            sems((X - 1, CHUNKS)),
            sems((Z,)),
            sems((Z,)),
            sems((X - 1,)),
            sems((X - 1,)),
        ],
        compiler_params=pltpu.CompilerParams(
            collective_id=0, has_side_effects=True, vmem_limit_bytes=48 * MIB
        ),
    )(queries, keys, values, node_table, parents, positions, out_weight, resid, gain)


def merge_tiles(tiles):
    peak = tiles[0]
    for tile in tiles[1:]:
        peak = jnp.maximum(peak, tile)
    raised = jnp.exp(tiles[0] - peak)
    added = tiles[0]
    for tile in tiles[1:]:
        raised = raised + jnp.exp(tile - peak)
        added = added + tile
    return jnp.where(iota(peak.shape, 0) == 0, peak + jnp.log(raised), added)


def head_body(
    row_ref, w_hbm, node_ref, par_ref, pos_ref, leaf_ref, target_ref, old_ref, adv_ref,
    token_ref, leaf_out, loss_ref,
    w, part_a, part_b, part_c, logits, tiny, info, info_x, info_z, info_y,
    stat_s, stat_y, stat_x, stat_z, mine, mine_x, mine_z, last_s, last_r,
    w_sem, w_ss, w_rs, g_ss, g_rs, i_ss, i_rs, t_ss, t_rs, l_ss, l_rs,
):
    grp = lax.axis_index("grp")
    me = lax.axis_index("seg")
    y = grp // 2
    core = lax.rem(grp, 2)
    z = me // X
    x = lax.rem(me, X)
    at = {"x": x, "y": y, "z": z}
    size = {"x": X, "y": Y, "z": Z}

    def peer(axis, delta):
        moved = dict(at)
        moved[axis] = lax.rem(at[axis] + delta + size[axis], size[axis])
        return {"grp": moved["y"] * 2 + core, "seg": moved["z"] * X + moved["x"]}

    own_w = pltpu.make_async_copy(w_hbm, w.at[:, 0:VOC], w_sem)
    own_w.start()
    barrier = pltpu.get_barrier_semaphore()
    partners = [peer(axis, delta) for axis in "xyz" for delta in range(1, size[axis])]
    for delta in range(Y):
        partners.append({"grp": lax.rem(y + delta, Y) * 2 + 1 - core, "seg": me})
    for partner in partners:
        pl.semaphore_signal(barrier, 1, device_id=partner)

    bufs = (part_a, part_b, part_c)
    for (offset, width, order), buf in zip(PARTS, bufs):
        buf[x, y, z] = row_ref[:, offset : offset + width]
    tile_sub = iota((8, ROWS), 0)
    tile_lane = iota((8, ROWS), 1)
    tiny[...] = jnp.zeros_like(tiny)
    tiny[0:1, 0:SCORE] = target_ref[...].astype(F32)
    tiny[1:2, 0:SCORE] = old_ref[...]
    tiny[2:3, 0:2] = adv_ref[...]
    start = tiny[...]
    info[...] = jnp.where(
        tile_sub < 2, pltpu.roll(start, SCORE * me, 1), pltpu.roll(start, 2 * me, 1)
    )
    pl.semaphore_wait(barrier, len(partners))

    pending = []
    swap = pltpu.make_async_remote_copy(
        src_ref=w_hbm,
        dst_ref=w.at[:, VOC : 2 * VOC],
        send_sem=w_ss,
        recv_sem=w_rs,
        device_id={"grp": y * 2 + 1 - core, "seg": me},
    )

    def spread(axis, sources, into, base, ss, rs):
        count = size[axis]
        here = at[axis]
        for delta in range(1, count):
            there = lax.rem(here + delta, count)
            copy = pltpu.make_async_remote_copy(
                src_ref=sources(there),
                dst_ref=into.at[here],
                send_sem=ss.at[base + delta],
                recv_sem=rs.at[base + here],
                device_id=peer(axis, delta),
            )
            copy.start()
            pending.append(copy)

    def collect(axis, into, base, ss, rs):
        count = size[axis]
        here = at[axis]
        for delta in range(1, count):
            there = lax.rem(here + delta, count)
            pltpu.make_async_remote_copy(
                src_ref=into.at[there],
                dst_ref=into.at[there],
                send_sem=ss.at[base + delta],
                recv_sem=rs.at[base + there],
                device_id=peer(axis, delta),
            ).wait_recv()

    def gather(part, buf, order):
        ready = []
        for stage, axis in enumerate(order):
            count = size[axis]
            done = order[:stage]

            def block(index, half):
                where = []
                for name in "xyz":
                    if name == axis:
                        where.append(lax.rem(index + 2 * count, count))
                    elif name not in done:
                        where.append(at[name])
                    elif half is not None and name == done[0]:
                        cut = size[name] // 2
                        where.append(pl.ds(half * cut, cut))
                    else:
                        where.append(slice(None))
                return buf.at[tuple(where)]

            def ring(step, way):
                half = None
                if step == count // 2:
                    if stage == 0:
                        if way < 0:
                            return None
                    else:
                        half = 0 if way > 0 else 1
                index = ((part * 3 + stage) * 4 + step - 1) * 2 + (way < 0)
                sent = block(at[axis] - way * (step - 1), half)
                landed = block(at[axis] - way * step, half)
                send = pltpu.make_async_remote_copy(
                    src_ref=sent,
                    dst_ref=sent,
                    send_sem=g_ss.at[index],
                    recv_sem=g_rs.at[index],
                    device_id=peer(axis, way),
                )
                arrive = pltpu.make_async_remote_copy(
                    src_ref=landed,
                    dst_ref=landed,
                    send_sem=g_ss.at[index],
                    recv_sem=g_rs.at[index],
                    device_id=peer(axis, way),
                )
                return send, arrive

            for step in range(1, count // 2 + 1):
                for copy in ready:
                    copy.wait_recv()
                ready = []
                for way in (1, -1):
                    both = ring(step, way)
                    if both is not None:
                        both[0].start()
                        pending.append(both[0])
                        ready.append(both[1])
                yield
        for copy in ready:
            copy.wait_recv()

    def tell():
        info_x[x] = info[...]
        spread("x", lambda there: info_x.at[x], info_x, 0, i_ss, i_rs)
        yield
        yield
        collect("x", info_x, 0, i_ss, i_rs)
        info_z[z] = info_x[0] + info_x[1] + info_x[2] + info_x[3]
        spread("z", lambda there: info_z.at[z], info_z, X, i_ss, i_rs)
        yield
        yield
        collect("z", info_z, X, i_ss, i_rs)
        whole = info_z[0]
        for index in range(1, Z):
            whole = whole + info_z[index]
        info_y[y] = whole
        spread("y", lambda there: info_y.at[y], info_y, X + Z, i_ss, i_rs)
        yield
        yield
        collect("y", info_y, X + Z, i_ss, i_rs)

    running = [
        gather(part, buf, order) for part, ((offset, width, order), buf) in enumerate(zip(PARTS, bufs))
    ]
    running.append(tell())
    first = True
    while running:
        for item in list(running):
            try:
                next(item)
            except StopIteration:
                running.remove(item)
        if first:
            swap.start()
            first = False

    own_w.wait()
    swap.wait_recv()

    def columns(n, carry):
        cols = pl.ds(pl.multiple_of(256 * n, 256), 256)
        total = None
        for (offset, width, order), buf in zip(PARTS, bufs):
            for index in range(X):
                rows = buf[index].reshape(Y * Z * 16, width)
                term = mm(rows, w[DX * index + offset : DX * index + offset + width, cols])
                total = term if total is None else total + term
        logits[:, cols] = total
        return carry

    lax.fori_loop(0, 2 * VOC // 256, columns, 0)

    voc_lane = iota((ROWS, 2 * VOC), 1)
    own_base = (grp * SEG + me) * VOC
    other_base = ((2 * y + 1 - core) * SEG + me) * VOC - VOC
    voc_id = (voc_lane + jnp.where(voc_lane < VOC, own_base, other_base)).astype(F32)
    targets = jnp.concatenate(
        [info_y[...].reshape(8 * Y, ROWS), jnp.zeros((ROWS - 8 * Y, ROWS), F32)], axis=0
    ).T
    square_lane = iota((ROWS, ROWS), 1)
    for index in range(Y):
        block = logits[ROWS * index : ROWS * index + ROWS, :]
        top = jnp.max(block, axis=1, keepdims=True)
        lse = top + jnp.log(jnp.sum(jnp.exp(block - top), axis=1, keepdims=True))
        found = voc_id == targets[:, 8 * index : 8 * index + 1]
        picked = jnp.sum(jnp.where(found, block, 0.0), axis=1, keepdims=True)
        both = jnp.where(square_lane == 0, lse, jnp.where(square_lane == 1, picked, 0.0))
        stat_s[index] = both.T[0:8]
    spread("y", lambda there: stat_s.at[there], stat_y, 0, t_ss, t_rs)
    stat_y[y] = stat_s[y]

    closure_t = closure_transposed(par_ref[...])
    node_row = scored_nodes(node_ref[...], pos_ref[...])
    sub = iota((NODES, ROWS), 0)
    row_hot_t = hot(sub.astype(F32) == node_row)
    leaf_sub = iota((NODES, LEAVES), 0)
    leaf_hot_t = hot(leaf_sub == leaf_ref[...])
    leaf_reach_t = mm(closure_t, leaf_hot_t)
    leaf_reach = jnp.concatenate([leaf_reach_t, jnp.zeros((NODES, NODES - LEAVES), F32)], axis=1).T
    path = mm(leaf_reach.astype(BF16), row_hot_t)
    counts = jnp.maximum(jnp.sum(path, axis=1, keepdims=True), 1.0)

    collect("y", stat_y, 0, t_ss, t_rs)
    mine[...] = merge_tiles([stat_y[index] for index in range(Y)])
    spread("x", lambda there: mine, stat_x, Y, t_ss, t_rs)
    stat_x[x] = mine[...]
    collect("x", stat_x, Y, t_ss, t_rs)
    mine_x[...] = merge_tiles([stat_x[index] for index in range(X)])
    spread("z", lambda there: mine_x, stat_z, Y + X, t_ss, t_rs)
    stat_z[z] = mine_x[...]
    collect("z", stat_z, Y + X, t_ss, t_rs)
    merged = merge_tiles([stat_z[index] for index in range(Z)])

    own_info = info_y[y]
    token_row = merged[1:2] - merged[0:1] - own_info[1:2]
    shift = lax.rem(ROWS - SCORE * me, ROWS)
    token_ref[...] = pltpu.roll(jnp.broadcast_to(token_row, (8, ROWS)), shift, 1)[0:1, 0:SCORE]
    means = jnp.sum(path * token_row, axis=1, keepdims=True) / counts
    leaf_row = jnp.broadcast_to(means, (ROWS, ROWS)).T[0:8]
    leaf_out[...] = pltpu.roll(leaf_row, lax.rem(ROWS - 2 * me, ROWS), 1)[0:1, 0:2]
    gains = own_info[2:3]
    ratio = jnp.exp(leaf_row)
    terms = jnp.minimum(ratio * gains, jnp.clip(ratio, 1.0 - EPS_LOW, 1.0 + EPS_HIGH) * gains)
    terms = jnp.where((tile_sub == 0) & (tile_lane < LEAVES), terms, 0.0)
    last_s[...] = terms

    last = []
    for delta in range(1, GRP):
        copy = pltpu.make_async_remote_copy(
            src_ref=last_s,
            dst_ref=last_r.at[grp],
            send_sem=l_ss.at[delta],
            recv_sem=l_rs.at[grp],
            device_id={"grp": lax.rem(grp + delta, GRP), "seg": me},
        )
        copy.start()
        last.append(copy)
    last_r[grp] = terms
    for delta in range(1, GRP):
        there = lax.rem(grp + delta, GRP)
        pltpu.make_async_remote_copy(
            src_ref=last_s,
            dst_ref=last_r.at[there],
            send_sem=l_ss.at[delta],
            recv_sem=l_rs.at[there],
            device_id={"grp": there, "seg": me},
        ).wait_recv()
    everything = last_r[0]
    for index in range(1, GRP):
        everything = everything + last_r[index]
    loss_ref[...] = -jnp.sum(everything, axis=(0, 1), keepdims=True) / (LEAVES * GRP)

    for copy in pending:
        copy.wait_send()
    swap.wait_send()
    for copy in last:
        copy.wait_send()


def head(rows, vocab_weight, node_table, parents, positions, leaf_node, targets, old_logp, advantages):
    sems = pltpu.SemaphoreType.DMA
    tile = pltpu.VMEM((8, ROWS), F32)

    def tiles(count):
        return pltpu.VMEM((count, 8, ROWS), F32)

    return pl.pallas_call(
        head_body,
        out_shape=(
            jax.ShapeDtypeStruct((1, SCORE), F32),
            jax.ShapeDtypeStruct((1, 2), F32),
            jax.ShapeDtypeStruct((1, 1), F32),
        ),
        in_specs=[vmem(), pl.BlockSpec(memory_space=pl.ANY)] + [vmem()] * 7,
        out_specs=(vmem(), vmem(), vmem()),
        scratch_shapes=[pltpu.VMEM((D, 2 * VOC), BF16)]
        + [pltpu.VMEM((X, Y, Z, 16, width), BF16) for offset, width, order in PARTS]
        + [
            pltpu.VMEM((Y * ROWS, 2 * VOC), F32),
            tile,
            tile,
            tiles(X),
            tiles(Z),
            tiles(Y),
            tiles(Y),
            tiles(Y),
            tiles(X),
            tiles(Z),
            tile,
            tile,
            tile,
            tile,
            tiles(GRP),
            sems,
            sems,
            sems,
            sems((72,)),
            sems((72,)),
            sems((X + Y + Z,)),
            sems((X + Y + Z,)),
            sems((X + Y + Z,)),
            sems((X + Y + Z,)),
            sems((GRP,)),
            sems((GRP,)),
        ],
        compiler_params=pltpu.CompilerParams(
            collective_id=1, has_side_effects=True, vmem_limit_bytes=56 * MIB
        ),
    )(rows, vocab_weight, node_table, parents, positions, leaf_node, targets, old_logp, advantages)


def body(
    queries, keys, values, node_ids, parents, score_pos, out_weight, resid, norm_gain,
    vocab_weight, targets, old_logp, leaf_node, advantages,
):
    node_table = node_ids.reshape(SEG, TOK)
    rows = attend(
        queries[0], keys[0], values[0], node_table, parents, score_pos, out_weight, resid[0],
        norm_gain.reshape(1, D),
    )
    token, leaf, loss = head(
        rows, vocab_weight, node_table, parents, score_pos, leaf_node, targets, old_logp, advantages
    )
    return (token, leaf, loss.reshape(()))


def solution(mesh):
    placed = (
        P("grp", "seg", None),
        P("grp", "seg", None),
        P("grp", "seg", None),
        P("grp", None),
        P("grp", None),
        P("grp", None),
        P("seg", None),
        P("grp", "seg", None),
        P(),
        P(None, ("grp", "seg")),
        P("grp", "seg"),
        P("grp", "seg"),
        P("grp", None),
        P("grp", "seg"),
    )
    return jax.shard_map(
        body,
        mesh=mesh,
        in_specs=placed,
        out_specs=(P("grp", "seg"), P("grp", "seg"), P()),
        check_vma=False,
    )
```

```python
import jax
import jax.numpy as jnp
from jax import lax
from jax.experimental import pallas as pl
from jax.experimental.pallas import tpu as pltpu
from jax.sharding import PartitionSpec as P

F32 = jnp.float32
BF16 = jnp.bfloat16
EPS_LOW = 0.0003
EPS_HIGH = 0.0004
NEGATIVE = -1e30
HEAD = 128
KV_HEADS = 8
X, Y, Z = 4, 4, 8
SEG = X * Z
GRP = 2 * Y
TOK = 128
ROWS = 128
NODES = 128
LEAVES = 64
SCORE = 4
WINDOW = 7
SLOTS = 8
OWNERS = X - 1 + WINDOW
D = 5120
DX = D // X
VOC = 384
PARTS = ((0, 512, "xyz"), (512, 384, "yzx"), (896, 384, "zxy"))
MIB = 1024 * 1024


def iota(shape, dim):
    return lax.broadcasted_iota(jnp.int32, shape, dim)


def hot(mask):
    return mask.astype(F32).astype(BF16)


def mm(a, b):
    return jnp.dot(a, b, preferred_element_type=F32)


def mm_nt(a, b):
    return lax.dot_general(a, b, (((1,), (1,)), ((), ())), preferred_element_type=F32)


def closure_transposed(parent_row):
    sub = iota((NODES, NODES), 0)
    lane = iota((NODES, NODES), 1)
    step = jnp.where((sub == parent_row) | (sub == lane), 1.0, 0.0)
    for squaring in range(3):
        half = step.astype(BF16)
        step = jnp.minimum(mm(half, half), 1.0)
    return step.astype(BF16)


def scored_nodes(node_table, position_row):
    table = jnp.concatenate([node_table.astype(F32), jnp.zeros((TOK - SEG, TOK), F32)], axis=0)
    across = table.T.astype(BF16)
    sub = iota((TOK, ROWS), 0)
    lane = iota((TOK, ROWS), 1)
    spread = mm(across, hot(sub == lane // SCORE))
    match = sub == position_row - TOK * (lane // SCORE)
    return jnp.sum(jnp.where(match, spread, 0.0), axis=0, keepdims=True)


def front(
    me, grp, q_ref, k_ref, v_ref, node_ref, par_ref, pos_ref, ow_hbm, resid_ref, gain_ref,
    qbuf, raised, parts, factors, osend, oxr, ozs, ozr, mixs, mixr, wown, wx, rsend, rrecv,
    zsend, zown, zrecv, sqs, sqr,
    w_sem, q_ss, q_rs, p_ss, p_rs, ox_ss, ox_rs, oz_ss, oz_rs, m_ss, m_rs, wx_ss, wx_rs, wy_ss, wy_rs,
    r_ss, r_rs, z_ss, z_rs, s_ss, s_rs, greet, early, middle,
):
    z = me // X
    x = lax.rem(me, X)
    pending = []

    def at_x(delta):
        return {"seg": z * X + lax.rem(x + delta, X)}

    def at_z(delta):
        return {"seg": lax.rem(z + delta, Z) * X + x}

    def send(src, dst, ss, rs, device):
        copy = pltpu.make_async_remote_copy(
            src_ref=src, dst_ref=dst, send_sem=ss, recv_sem=rs, device_id=device
        )
        copy.start()
        pending.append(copy)

    def landed(dst, ss, rs, device):
        pltpu.make_async_remote_copy(
            src_ref=dst, dst_ref=dst, send_sem=ss, recv_sem=rs, device_id=device
        ).wait_recv()

    def dx_cols(at):
        return pl.ds(pl.multiple_of(DX * at, DX), DX)

    own_weight = pltpu.make_async_copy(ow_hbm.at[:, dx_cols(x)], wown, w_sem)
    own_weight.start()
    for pair in range(SEG // 2):
        spot = []
        for half in range(2):
            h = 2 * pair + half
            spot += [
                q_ref[:, HEAD * (2 * h + piece) : HEAD * (2 * h + piece + 1)].astype(F32)
                for piece in range(2)
            ]
        k = pair // 2
        row = HEAD * (k % 2) + 32 * (k // 2) + 16 * (pair % 2)
        qbuf[0, row : row + 16, :] = jnp.concatenate(spot, axis=0).astype(BF16)
    qbuf[WINDOW] = jnp.zeros((2 * ROWS, HEAD), BF16)
    greet()

    for c in range(2):
        rows = pl.ds(HEAD * c, HEAD)
        for slot in range(1, WINDOW):
            send(
                qbuf.at[0, rows],
                qbuf.at[slot, rows],
                q_ss.at[c, slot],
                q_rs.at[c, slot],
                {"seg": lax.rem(me - slot + SEG, SEG)},
            )

    slab = pl.ds(pl.multiple_of(32 * grp, 32), 32)
    for delta in range(1, X):
        send(
            ow_hbm.at[slab, dx_cols(lax.rem(x + delta, X))],
            wx.at[delta - 1, slab],
            wx_ss.at[delta - 1],
            wx_rs.at[delta - 1],
            at_x(delta),
        )
    early()

    place_row = iota((16, 16), 0)
    place_col = iota((16, 16), 1)
    place = hot((place_row == SCORE * x + place_col) & (place_col < SCORE))
    for delta in range(X):
        cols = resid_ref[:, dx_cols(lax.rem(x + delta, X))]
        padded = jnp.concatenate([cols.astype(F32), jnp.zeros((16 - SCORE, DX), F32)], axis=0)
        rsend[delta] = mm(place, padded.astype(BF16)).astype(BF16)
        if delta:
            send(rsend.at[delta], rrecv.at[delta - 1], r_ss.at[delta], r_rs.at[delta], at_x(delta))

    closure_t = closure_transposed(par_ref[...])
    position_row = pos_ref[...]
    node_row = scored_nodes(node_ref[...], position_row)
    sub = iota((NODES, ROWS), 0)
    row_hot_t = hot(sub.astype(F32) == node_row)
    reach_t = mm(closure_t, row_hot_t).astype(BF16)
    own_nodes = node_ref[pl.ds(me, 1), :]
    token_hot = jnp.where(sub == own_nodes, 1.0, 0.0).T.astype(BF16)
    linked = mm(token_hot, reach_t)
    visible = hot((linked > 0.5) & (sub + TOK * me <= position_row))
    wide_sub = iota((ROWS, 2 * ROWS), 0)
    wide_lane = iota((ROWS, 2 * ROWS), 1)
    wanted = lax.rem(SCORE * (me + wide_lane // 32) + lax.rem(wide_lane, SCORE), ROWS)
    mask = mm(visible, hot((wide_sub == wanted) & (wide_lane < 32 * WINDOW))) > 0.5

    scale = HEAD ** (-0.5)
    for c in range(2):
        for slot in range(1, WINDOW):
            landed(
                qbuf.at[slot, pl.ds(HEAD * c, HEAD)],
                q_ss.at[c, slot],
                q_rs.at[c, slot],
                {"seg": lax.rem(me + slot, SEG)},
            )
        for i in range(4):
            k = 2 * i + c
            row = HEAD * c + 32 * i
            query = qbuf[:, row : row + 32, :].reshape(2 * ROWS, HEAD)
            lanes = slice(HEAD * k, HEAD * k + HEAD)
            scores = jnp.where(mask, mm_nt(k_ref[:, lanes], query) * scale, NEGATIVE)
            top = jnp.max(scores, axis=0, keepdims=True)
            power = jnp.where(mask, jnp.exp(scores - top), 0.0)
            raised[4 * c + i] = power
            parts[c, WINDOW - 1, i : i + 1, :] = top
            parts[c, WINDOW - 1, 4 + i : 5 + i, :] = jnp.sum(power, axis=0, keepdims=True)
        for delta in range(1, WINDOW):
            for way in (delta, -delta):
                slot = WINDOW - 1 - way
                send(
                    parts.at[c, WINDOW - 1],
                    parts.at[c, slot],
                    p_ss.at[c, slot],
                    p_rs.at[c, slot],
                    {"seg": lax.rem(me + way + SEG, SEG)},
                )

    for delta in range(1, X):
        landed(wx.at[delta - 1, slab], wx_ss.at[delta - 1], wx_rs.at[delta - 1], at_x(delta))
    for delta in range(1, GRP):
        send(
            wx.at[:, slab],
            wx.at[:, slab],
            wy_ss.at[delta],
            wy_rs.at[grp],
            {"grp": lax.rem(grp + delta, GRP), "seg": me},
        )

    part_slot = iota((4, 2 * ROWS), 1) // 32
    for c in range(2):
        tops = []
        totals = []
        for away in range(1 - WINDOW, WINDOW):
            slot = away + WINDOW - 1
            if away != 0:
                landed(
                    parts.at[c, slot],
                    p_ss.at[c, slot],
                    p_rs.at[c, slot],
                    {"seg": lax.rem(me + away + SEG, SEG)},
                )
            value = parts[c, slot]
            if away != 0:
                value = pltpu.roll(value, (32 * away) % (2 * ROWS), 1)
            valid = (part_slot >= away) & (part_slot < away + WINDOW)
            tops.append(jnp.where(valid, value[0:4], NEGATIVE))
            totals.append(jnp.where(valid, value[4:8], 0.0))
        peak = tops[0]
        for top in tops[1:]:
            peak = jnp.maximum(peak, top)
        whole = totals[0] * jnp.exp(tops[0] - peak)
        for top, total in zip(tops[1:], totals[1:]):
            whole = whole + total * jnp.exp(top - peak)
        own_top = parts[c, WINDOW - 1][0:4]
        factors[c, 0:4, :] = jnp.exp(own_top - peak) / jnp.where(whole > 0.0, whole, 1.0)
        for step in range(4):
            i = lax.rem(z // 2 + step, 4)
            at = 4 * c + i
            lanes = pl.ds(pl.multiple_of(HEAD * (2 * i + c), HEAD), HEAD)
            probs = raised[at] * factors[c, pl.ds(i, 1), :]
            mixed = mm(probs.T.astype(BF16), v_ref[:, lanes]).reshape(SLOTS, 4, 8, HEAD)
            for pair in range(4):
                osend[at, pair] = mixed[0:WINDOW, pair].reshape(8 * WINDOW, HEAD)
            for delta in (1, 3, 2):
                send(
                    osend.at[at, lax.rem(x + delta, X)],
                    oxr.at[at, delta - 1],
                    ox_ss.at[4 * c + step, delta - 1],
                    ox_rs.at[at, delta - 1],
                    at_x(delta),
                )

    guarded = []
    for c in range(2):
        for step in range(4):
            i = lax.rem(z // 2 + step, 4)
            at = 4 * c + i
            target = 2 * i + c
            for delta in (1, 3, 2):
                landed(
                    oxr.at[at, delta - 1],
                    ox_ss.at[4 * c + step, delta - 1],
                    ox_rs.at[at, delta - 1],
                    at_x(delta),
                )
            ozs[at] = jnp.zeros((8 * OWNERS, HEAD), F32)
            ozs[at, pl.ds(pl.multiple_of(8 * x, 8), 8 * WINDOW), :] = osend[at, x]
            for delta in range(1, X):
                span = pl.ds(pl.multiple_of(8 * lax.rem(x - delta + X, X), 8), 8 * WINDOW)
                ozs[at, span, :] = ozs[at, span, :] + oxr[at, delta - 1]
            away_copy = pltpu.make_async_remote_copy(
                src_ref=ozs.at[at],
                dst_ref=ozr.at[z],
                send_sem=oz_ss.at[4 * c + step],
                recv_sem=oz_rs.at[z],
                device_id={"seg": target * X + x},
            )
            if step == 0:
                guarded.append((target, away_copy))

                @pl.when(target == z)
                def _():
                    ozr[z] = ozs[at]

                @pl.when(target != z)
                def _():
                    away_copy.start()

            else:
                away_copy.start()
                pending.append(away_copy)

    middle(closure_t, row_hot_t)

    for delta in range(1, Z):
        source = lax.rem(z + delta, Z)
        landed(ozr.at[source], oz_ss.at[0], oz_rs.at[source], at_z(delta))
    sums = [None] * SEG
    for source in range(Z):
        block = ozr[source]
        for slot in range(OWNERS):
            row = X * source + slot
            if row < SEG:
                term = block[8 * slot : 8 * slot + 8]
                sums[row] = term if sums[row] is None else sums[row] + term
    stacked = jnp.concatenate(sums, axis=0).astype(BF16)
    out_row = iota((2 * ROWS, 2 * ROWS), 0)
    in_row = iota((2 * ROWS, 2 * ROWS), 1)
    packed = lax.rem(out_row, ROWS)
    from_row = 8 * (packed // SCORE) + SCORE * (out_row // ROWS) + lax.rem(packed, SCORE)
    sorted_rows = mm(hot(in_row == from_row), stacked).astype(BF16)
    left = jnp.concatenate([sorted_rows[0:ROWS], sorted_rows[ROWS : 2 * ROWS]], axis=1)
    mixs[...] = left
    for delta in (1, 3, 2):
        send(mixs, mixr.at[delta - 1], m_ss.at[delta - 1], m_rs.at[delta - 1], at_x(delta))
    own_weight.wait()
    product = mm(left, wown[...])
    for delta in range(1, GRP):
        other = lax.rem(grp + delta, GRP)
        theirs = pl.ds(pl.multiple_of(32 * other, 32), 32)
        landed(wx.at[:, theirs], wy_ss.at[delta], wy_rs.at[other], {"grp": other, "seg": me})
    for delta in (1, 3, 2):
        landed(mixr.at[delta - 1], m_ss.at[delta - 1], m_rs.at[delta - 1], at_x(delta))
        product = product + mm(mixr[delta - 1], wx[delta - 1])
    zown[...] = product

    for delta in (1, 7, 2, 6, 3, 5, 4):
        target = lax.rem(z + delta, Z)
        zsend[delta] = encode(zown[pl.ds(pl.multiple_of(16 * target, 16), 16), :])
        send(zsend.at[delta], zrecv.at[delta], z_ss.at[delta], z_rs.at[delta], at_z(delta))
    hidden = zown[pl.ds(pl.multiple_of(16 * z, 16), 16), :] + rsend[0].astype(F32)
    for delta in range(1, X):
        landed(rrecv.at[delta - 1], r_ss.at[delta], r_rs.at[delta], at_x(delta))
        hidden = hidden + rrecv[delta - 1].astype(F32)
    for delta in (1, 7, 2, 6, 3, 5, 4):
        landed(zrecv.at[delta], z_ss.at[delta], z_rs.at[delta], at_z(delta))
        hidden = hidden + decode(zrecv[delta])
    squares = jnp.sum(hidden * hidden, axis=1, keepdims=True)
    sqs[...] = jnp.broadcast_to(squares, sqs.shape)
    for delta in (1, 3, 2):
        send(sqs, sqr.at[delta - 1], s_ss.at[delta - 1], s_rs.at[delta - 1], at_x(delta))
    gain = gain_ref[:, dx_cols(x)].astype(F32)
    for delta in (1, 3, 2):
        landed(sqr.at[delta - 1], s_ss.at[delta - 1], s_rs.at[delta - 1], at_x(delta))
    power = (sqs[...] + sqr[0] + sqr[1] + sqr[2])[:, 0:1] / D
    normed = (hidden * lax.rsqrt(power + 1e-06) * gain).astype(BF16)

    def drain():
        for copy in pending:
            copy.wait_send()
        for target, copy in guarded:

            @pl.when(target != z)
            def _():
                copy.wait_send()

    return normed, drain


def front_scratch():
    sems = pltpu.SemaphoreType.DMA
    return [
        pltpu.VMEM((SLOTS, 2 * ROWS, HEAD), BF16),
        pltpu.VMEM((KV_HEADS, TOK, 2 * ROWS), F32),
        pltpu.VMEM((2, 2 * WINDOW - 1, 8, 2 * ROWS), F32),
        pltpu.VMEM((2, 8, 2 * ROWS), F32),
        pltpu.VMEM((KV_HEADS, X, 8 * WINDOW, HEAD), F32),
        pltpu.VMEM((KV_HEADS, X - 1, 8 * WINDOW, HEAD), F32),
        pltpu.VMEM((KV_HEADS, 8 * OWNERS, HEAD), F32),
        pltpu.VMEM((Z, 8 * OWNERS, HEAD), F32),
        pltpu.VMEM((ROWS, 2 * HEAD), BF16),
        pltpu.VMEM((X - 1, ROWS, 2 * HEAD), BF16),
        pltpu.VMEM((2 * HEAD, DX), BF16),
        pltpu.VMEM((X - 1, 2 * HEAD, DX), BF16),
        pltpu.VMEM((X, 16, DX), BF16),
        pltpu.VMEM((X - 1, 16, DX), BF16),
        pltpu.VMEM((Z, 16, DX + HEAD), jnp.int16),
        pltpu.VMEM((ROWS, DX), F32),
        pltpu.VMEM((Z, 16, DX + HEAD), jnp.int16),
        pltpu.VMEM((16, HEAD), F32),
        pltpu.VMEM((X - 1, 16, HEAD), F32),
        sems,
        sems((2, WINDOW)),
        sems((2, WINDOW)),
        sems((2, 2 * WINDOW - 1)),
        sems((2, 2 * WINDOW - 1)),
        sems((KV_HEADS, X - 1)),
        sems((KV_HEADS, X - 1)),
        sems((Z,)),
        sems((Z,)),
        sems((X - 1,)),
        sems((X - 1,)),
        sems((X - 1,)),
        sems((X - 1,)),
        sems((GRP,)),
        sems((GRP,)),
        sems((X,)),
        sems((X,)),
        sems((Z,)),
        sems((Z,)),
        sems((X - 1,)),
        sems((X - 1,)),
    ]


def encode(value):
    most = jnp.maximum(jnp.max(jnp.abs(value), axis=1, keepdims=True), 1e-30)
    level = jnp.ceil(jnp.log2(most * (1.0 / 32000.0)))
    scaled = jnp.round(value * jnp.exp2(-level)).astype(jnp.int32)
    levels = jnp.broadcast_to(level.astype(jnp.int32), (value.shape[0], HEAD))
    return jnp.concatenate([scaled, levels], axis=1).astype(jnp.int16)


def decode(code):
    wide = code.astype(jnp.int32).astype(F32)
    return wide[:, 0:DX] * jnp.exp2(wide[:, DX : DX + 1])


def vmem():
    return pl.BlockSpec(memory_space=pltpu.VMEM)


def merge_tiles(tiles):
    peak = tiles[0]
    for tile in tiles[1:]:
        peak = jnp.maximum(peak, tile)
    raised = jnp.exp(tiles[0] - peak)
    added = tiles[0]
    for tile in tiles[1:]:
        raised = raised + jnp.exp(tile - peak)
        added = added + tile
    return jnp.where(iota(peak.shape, 0) == 0, peak + jnp.log(raised), added)


def program_body(
    q_hbm, k_hbm, v_hbm, node_hbm, par_hbm, pos_hbm, ow_hbm, resid_hbm, gain_ref,
    w_hbm, leaf_hbm, target_hbm, old_hbm, adv_hbm,
    token_ref, leaf_out, loss_ref,
    q_ref, k_ref, v_ref, node_ref, par_ref, pos_ref, resid_ref, leaf_ref, target_ref, old_ref, adv_ref,
    in_sems, *rest,
):
    front_count = len(front_scratch())
    front_refs = rest[:front_count]
    (
        w, part_a, part_b, part_c, logits, paths, tiny, info, info_x, info_z, info_y,
        stat_s, stat_y, stat_x, stat_z, mine, mine_x, last_s, last_r,
        w_sem, w_ss, w_rs, g_ss, g_rs, i_ss, i_rs, t_ss, t_rs, l_ss, l_rs,
    ) = rest[front_count:]
    grp = lax.axis_index("grp")
    me = lax.axis_index("seg")
    y = grp // 2
    core = lax.rem(grp, 2)
    z = me // X
    x = lax.rem(me, X)
    at = {"x": x, "y": y, "z": z}
    size = {"x": X, "y": Y, "z": Z}

    def peer(axis, delta):
        moved = dict(at)
        moved[axis] = lax.rem(at[axis] + delta + size[axis], size[axis])
        return {"grp": moved["y"] * 2 + core, "seg": moved["z"] * X + moved["x"]}

    barrier = pltpu.get_barrier_semaphore()
    offsets = [way * delta for delta in range(1, WINDOW) for way in (1, -1)]
    offsets += [delta for delta in range(X, SEG, X) if min(delta, SEG - delta) >= WINDOW]
    partners = [{"seg": lax.rem(me + delta + SEG, SEG)} for delta in offsets]
    partners += [{"grp": lax.rem(grp + delta, GRP)} for delta in range(1, GRP)]
    for partner in partners:
        pl.semaphore_signal(barrier, 1, device_id=partner)
    loads = []
    for index, (src, dst) in enumerate(
        (
            (q_hbm, q_ref), (k_hbm, k_ref), (v_hbm, v_ref), (node_hbm, node_ref), (par_hbm, par_ref),
            (pos_hbm, pos_ref), (resid_hbm, resid_ref), (leaf_hbm, leaf_ref),
            (target_hbm, target_ref), (old_hbm, old_ref), (adv_hbm, adv_ref),
        )
    ):
        copy = pltpu.make_async_copy(src, dst, in_sems.at[index])
        copy.start()
        loads.append(copy)
    own_w = pltpu.make_async_copy(w_hbm, w.at[:, 0:VOC], w_sem)
    loads[0].wait()

    tile_sub = iota((8, ROWS), 0)
    tile_lane = iota((8, ROWS), 1)
    pending = []
    swap = pltpu.make_async_remote_copy(
        src_ref=w_hbm,
        dst_ref=w.at[:, VOC : 2 * VOC],
        send_sem=w_ss,
        recv_sem=w_rs,
        device_id={"grp": y * 2 + 1 - core, "seg": me},
    )

    def spread(axis, sources, into, base, ss, rs):
        count = size[axis]
        here = at[axis]
        for delta in range(1, count):
            there = lax.rem(here + delta, count)
            copy = pltpu.make_async_remote_copy(
                src_ref=sources(there),
                dst_ref=into.at[here],
                send_sem=ss.at[base + delta],
                recv_sem=rs.at[base + here],
                device_id=peer(axis, delta),
            )
            copy.start()
            pending.append(copy)

    def collect(axis, into, base, ss, rs):
        count = size[axis]
        here = at[axis]
        for delta in range(1, count):
            there = lax.rem(here + delta, count)
            pltpu.make_async_remote_copy(
                src_ref=into.at[there],
                dst_ref=into.at[there],
                send_sem=ss.at[base + delta],
                recv_sem=rs.at[base + there],
                device_id=peer(axis, delta),
            ).wait_recv()

    def gather(part, buf, order):
        ready = []
        for stage, axis in enumerate(order):
            count = size[axis]
            done = order[:stage]

            def block(index, half):
                where = []
                for name in "xyz":
                    if name == axis:
                        where.append(lax.rem(index + 2 * count, count))
                    elif name not in done:
                        where.append(at[name])
                    elif half is not None and name == done[0]:
                        cut = size[name] // 2
                        where.append(pl.ds(half * cut, cut))
                    else:
                        where.append(slice(None))
                return buf.at[tuple(where)]

            def ring(step, way):
                half = None
                if step == count // 2:
                    if stage == 0:
                        if way < 0:
                            return None
                    else:
                        half = 0 if way > 0 else 1
                index = ((part * 3 + stage) * 4 + step - 1) * 2 + (way < 0)
                sent = block(at[axis] - way * (step - 1), half)
                landed = block(at[axis] - way * step, half)
                send = pltpu.make_async_remote_copy(
                    src_ref=sent,
                    dst_ref=sent,
                    send_sem=g_ss.at[index],
                    recv_sem=g_rs.at[index],
                    device_id=peer(axis, way),
                )
                arrive = pltpu.make_async_remote_copy(
                    src_ref=landed,
                    dst_ref=landed,
                    send_sem=g_ss.at[index],
                    recv_sem=g_rs.at[index],
                    device_id=peer(axis, way),
                )
                return send, arrive

            for step in range(1, count // 2 + 1):
                for copy in ready:
                    copy.wait_recv()
                ready = []
                for way in (1, -1):
                    both = ring(step, way)
                    if both is not None:
                        both[0].start()
                        pending.append(both[0])
                        ready.append(both[1])
                yield
        for copy in ready:
            copy.wait_recv()

    def tell():
        tiny[...] = jnp.zeros_like(tiny)
        tiny[0:1, 0:SCORE] = target_ref[...].astype(F32)
        tiny[1:2, 0:SCORE] = old_ref[...]
        tiny[2:3, 0:2] = adv_ref[...]
        start = tiny[...]
        info[...] = jnp.where(
            tile_sub < 2, pltpu.roll(start, SCORE * me, 1), pltpu.roll(start, 2 * me, 1)
        )
        info_x[x] = info[...]
        spread("x", lambda there: info_x.at[x], info_x, 0, i_ss, i_rs)
        yield
        collect("x", info_x, 0, i_ss, i_rs)
        info_z[z] = info_x[0] + info_x[1] + info_x[2] + info_x[3]
        spread("z", lambda there: info_z.at[z], info_z, X, i_ss, i_rs)
        yield
        collect("z", info_z, X, i_ss, i_rs)
        whole = info_z[0]
        for index in range(1, Z):
            whole = whole + info_z[index]
        info_y[y] = whole
        spread("y", lambda there: info_y.at[y], info_y, X + Z, i_ss, i_rs)
        yield
        collect("y", info_y, X + Z, i_ss, i_rs)

    talk = tell()

    def greet():
        pl.semaphore_wait(barrier, len(partners))

    def early():
        own_w.start()
        swap.start()
        for copy in loads[1:]:
            copy.wait()
        next(talk)

    def middle(closure_t, row_hot_t):
        next(talk)
        leaf_hot_t = hot(iota((NODES, LEAVES), 0) == leaf_ref[...])
        leaf_reach_t = mm(closure_t, leaf_hot_t)
        filler = jnp.zeros((NODES, NODES - LEAVES), F32)
        leaf_reach = jnp.concatenate([leaf_reach_t, filler], axis=1).T
        paths[...] = mm(leaf_reach.astype(BF16), row_hot_t)

    normed, drain = front(
        me, grp, q_ref, k_ref, v_ref, node_ref, par_ref, pos_ref, ow_hbm, resid_ref, gain_ref,
        *front_refs, greet, early, middle,
    )
    bufs = (part_a, part_b, part_c)
    for (offset, width, order), buf in zip(PARTS, bufs):
        buf[x, y, z] = normed[:, offset : offset + width]
    next(talk)
    running = [
        gather(part, buf, order) for part, ((offset, width, order), buf) in enumerate(zip(PARTS, bufs))
    ]
    while running:
        for item in list(running):
            try:
                next(item)
            except StopIteration:
                running.remove(item)
    for rest_of in talk:
        pass

    own_w.wait()
    swap.wait_recv()

    def columns(n, carry):
        cols = pl.ds(pl.multiple_of(256 * n, 256), 256)
        total = None
        for (offset, width, order), buf in zip(PARTS, bufs):
            for index in range(X):
                rows = buf[index].reshape(Y * Z * 16, width)
                term = mm(rows, w[DX * index + offset : DX * index + offset + width, cols])
                total = term if total is None else total + term
        logits[:, cols] = total
        return carry

    lax.fori_loop(0, 2 * VOC // 256, columns, 0)

    voc_lane = iota((ROWS, 2 * VOC), 1)
    own_base = (grp * SEG + me) * VOC
    other_base = ((2 * y + 1 - core) * SEG + me) * VOC - VOC
    voc_id = (voc_lane + jnp.where(voc_lane < VOC, own_base, other_base)).astype(F32)
    targets = jnp.concatenate(
        [info_y[...].reshape(8 * Y, ROWS), jnp.zeros((ROWS - 8 * Y, ROWS), F32)], axis=0
    ).T
    square_lane = iota((ROWS, ROWS), 1)
    for index in range(Y):
        block = logits[ROWS * index : ROWS * index + ROWS, :]
        top = jnp.max(block, axis=1, keepdims=True)
        lse = top + jnp.log(jnp.sum(jnp.exp(block - top), axis=1, keepdims=True))
        found = voc_id == targets[:, 8 * index : 8 * index + 1]
        picked = jnp.sum(jnp.where(found, block, 0.0), axis=1, keepdims=True)
        both = jnp.where(square_lane == 0, lse, jnp.where(square_lane == 1, picked, 0.0))
        stat_s[index] = both.T[0:8]
    spread("y", lambda there: stat_s.at[there], stat_y, 0, t_ss, t_rs)
    stat_y[y] = stat_s[y]

    path = paths[...]
    counts = jnp.maximum(jnp.sum(path, axis=1, keepdims=True), 1.0)
    collect("y", stat_y, 0, t_ss, t_rs)
    mine[...] = merge_tiles([stat_y[index] for index in range(Y)])
    spread("x", lambda there: mine, stat_x, Y, t_ss, t_rs)
    stat_x[x] = mine[...]
    collect("x", stat_x, Y, t_ss, t_rs)
    mine_x[...] = merge_tiles([stat_x[index] for index in range(X)])
    spread("z", lambda there: mine_x, stat_z, Y + X, t_ss, t_rs)
    stat_z[z] = mine_x[...]
    collect("z", stat_z, Y + X, t_ss, t_rs)
    merged = merge_tiles([stat_z[index] for index in range(Z)])

    own_info = info_y[y]
    token_row = merged[1:2] - merged[0:1] - own_info[1:2]
    shift = lax.rem(ROWS - SCORE * me, ROWS)
    token_ref[...] = pltpu.roll(jnp.broadcast_to(token_row, (8, ROWS)), shift, 1)[0:1, 0:SCORE]
    means = jnp.sum(path * token_row, axis=1, keepdims=True) / counts
    leaf_row = jnp.broadcast_to(means, (ROWS, ROWS)).T[0:8]
    leaf_out[...] = pltpu.roll(leaf_row, lax.rem(ROWS - 2 * me, ROWS), 1)[0:1, 0:2]
    gains = own_info[2:3]
    ratio = jnp.exp(leaf_row)
    terms = jnp.minimum(ratio * gains, jnp.clip(ratio, 1.0 - EPS_LOW, 1.0 + EPS_HIGH) * gains)
    terms = jnp.where((tile_sub == 0) & (tile_lane < LEAVES), terms, 0.0)
    last_s[...] = terms

    last = []
    for delta in range(1, GRP):
        copy = pltpu.make_async_remote_copy(
            src_ref=last_s,
            dst_ref=last_r.at[grp],
            send_sem=l_ss.at[delta],
            recv_sem=l_rs.at[grp],
            device_id={"grp": lax.rem(grp + delta, GRP), "seg": me},
        )
        copy.start()
        last.append(copy)
    last_r[grp] = terms
    for delta in range(1, GRP):
        there = lax.rem(grp + delta, GRP)
        pltpu.make_async_remote_copy(
            src_ref=last_s,
            dst_ref=last_r.at[there],
            send_sem=l_ss.at[delta],
            recv_sem=l_rs.at[there],
            device_id={"grp": there, "seg": me},
        ).wait_recv()
    everything = last_r[0]
    for index in range(1, GRP):
        everything = everything + last_r[index]
    loss_ref[...] = -jnp.sum(everything, axis=(0, 1), keepdims=True) / (LEAVES * GRP)

    drain()
    for copy in pending:
        copy.wait_send()
    swap.wait_send()
    for copy in last:
        copy.wait_send()


def body(
    queries, keys, values, node_ids, parents, score_pos, out_weight, resid, norm_gain,
    vocab_weight, targets, old_logp, leaf_node, advantages,
):
    sems = pltpu.SemaphoreType.DMA
    tile = pltpu.VMEM((8, ROWS), F32)

    def tiles(count):
        return pltpu.VMEM((count, 8, ROWS), F32)

    anywhere = pl.BlockSpec(memory_space=pl.ANY)
    token, leaf, loss = pl.pallas_call(
        program_body,
        out_shape=(
            jax.ShapeDtypeStruct((1, SCORE), F32),
            jax.ShapeDtypeStruct((1, 2), F32),
            jax.ShapeDtypeStruct((1, 1), F32),
        ),
        in_specs=[anywhere] * 8 + [vmem()] + [anywhere] * 5,
        out_specs=(vmem(), vmem(), vmem()),
        scratch_shapes=[
            pltpu.VMEM((SCORE, 64 * HEAD), BF16),
            pltpu.VMEM((TOK, KV_HEADS * HEAD), BF16),
            pltpu.VMEM((TOK, KV_HEADS * HEAD), BF16),
            pltpu.VMEM((SEG, TOK), jnp.int32),
            pltpu.VMEM((1, NODES), jnp.int32),
            pltpu.VMEM((1, ROWS), jnp.int32),
            pltpu.VMEM((SCORE, D), BF16),
            pltpu.VMEM((1, LEAVES), jnp.int32),
            pltpu.VMEM((1, SCORE), jnp.int32),
            pltpu.VMEM((1, SCORE), F32),
            pltpu.VMEM((1, 2), F32),
            sems((11,)),
        ]
        + front_scratch()
        + [pltpu.VMEM((D, 2 * VOC), BF16)]
        + [pltpu.VMEM((X, Y, Z, 16, width), BF16) for offset, width, order in PARTS]
        + [
            pltpu.VMEM((Y * ROWS, 2 * VOC), F32),
            pltpu.VMEM((NODES, ROWS), F32),
            tile,
            tile,
            tiles(X),
            tiles(Z),
            tiles(Y),
            tiles(Y),
            tiles(Y),
            tiles(X),
            tiles(Z),
            tile,
            tile,
            tile,
            tiles(GRP),
            sems,
            sems,
            sems,
            sems((72,)),
            sems((72,)),
            sems((X + Y + Z,)),
            sems((X + Y + Z,)),
            sems((X + Y + Z,)),
            sems((X + Y + Z,)),
            sems((GRP,)),
            sems((GRP,)),
        ],
        compiler_params=pltpu.CompilerParams(
            collective_id=0, has_side_effects=True, vmem_limit_bytes=58 * MIB
        ),
    )(
        queries[0], keys[0], values[0], node_ids.reshape(SEG, TOK), parents, score_pos, out_weight,
        resid[0], norm_gain.reshape(1, D), vocab_weight, leaf_node, targets, old_logp, advantages,
    )
    return (token, leaf, loss.reshape(()))


def solution(mesh):
    placed = (
        P("grp", "seg", None),
        P("grp", "seg", None),
        P("grp", "seg", None),
        P("grp", None),
        P("grp", None),
        P("grp", None),
        P("seg", None),
        P("grp", "seg", None),
        P(),
        P(None, ("grp", "seg")),
        P("grp", "seg"),
        P("grp", "seg"),
        P("grp", None),
        P("grp", "seg"),
    )
    return jax.shard_map(
        body,
        mesh=mesh,
        in_specs=placed,
        out_specs=(P("grp", "seg"), P("grp", "seg"), P()),
        check_vma=False,
    )
```

```python
import jax
import jax.numpy as jnp
from jax import lax
from jax.experimental import pallas as pl
from jax.experimental.pallas import tpu as pltpu
from jax.sharding import PartitionSpec as P

F32 = jnp.float32
BF16 = jnp.bfloat16
EPS_LOW = 0.0003
EPS_HIGH = 0.0004
NEGATIVE = -1e30
HEAD = 128
KV_HEADS = 8
X, Y, Z = 4, 4, 8
SEG = X * Z
GRP = 2 * Y
TOK = 128
ROWS = 128
NODES = 128
LEAVES = 64
SCORE = 4
WINDOW = 7
SLOTS = 8
OWNERS = X - 1 + WINDOW
D = 5120
DX = D // X
VOC = 384
PARTS = ((0, 384, "yxz"), (384, 512, "yzx"), (896, 384, "zxy"))
MIB = 1024 * 1024


def iota(shape, dim):
    return lax.broadcasted_iota(jnp.int32, shape, dim)


def hot(mask):
    return mask.astype(F32).astype(BF16)


def mm(a, b):
    return jnp.dot(a, b, preferred_element_type=F32)


def mm_nt(a, b):
    return lax.dot_general(a, b, (((1,), (1,)), ((), ())), preferred_element_type=F32)


def closure_transposed(parent_row):
    sub = iota((NODES, NODES), 0)
    lane = iota((NODES, NODES), 1)
    step = jnp.where((sub == parent_row) | (sub == lane), 1.0, 0.0)
    for squaring in range(3):
        half = step.astype(BF16)
        step = jnp.minimum(mm(half, half), 1.0)
    return step.astype(BF16)


def scored_nodes(node_table, position_row):
    table = jnp.concatenate([node_table.astype(F32), jnp.zeros((TOK - SEG, TOK), F32)], axis=0)
    across = table.T.astype(BF16)
    sub = iota((TOK, ROWS), 0)
    lane = iota((TOK, ROWS), 1)
    spread = mm(across, hot(sub == lane // SCORE))
    match = sub == position_row - TOK * (lane // SCORE)
    return jnp.sum(jnp.where(match, spread, 0.0), axis=0, keepdims=True)


def front(
    me, grp, q_ref, k_ref, v_ref, node_ref, par_ref, pos_ref, ow_hbm, resid_ref, gain_ref,
    qbuf, raised, parts, factors, osend, oxr, ozs, ozr, mixs, mixr, wown, wx, rsend, rrecv,
    zsend, zown, zrecv, sqs, sqr,
    w_sem, q_ss, q_rs, p_ss, p_rs, ox_ss, ox_rs, oz_ss, oz_rs, m_ss, m_rs, wx_ss, wx_rs, wy_ss, wy_rs,
    r_ss, r_rs, z_ss, z_rs, s_ss, s_rs, greet, early, middle,
):
    z = me // X
    x = lax.rem(me, X)
    pending = []

    def at_x(delta):
        return {"seg": z * X + lax.rem(x + delta, X)}

    def at_z(delta):
        return {"seg": lax.rem(z + delta, Z) * X + x}

    def send(src, dst, ss, rs, device):
        copy = pltpu.make_async_remote_copy(
            src_ref=src, dst_ref=dst, send_sem=ss, recv_sem=rs, device_id=device
        )
        copy.start()
        pending.append(copy)

    def landed(dst, ss, rs, device):
        pltpu.make_async_remote_copy(
            src_ref=dst, dst_ref=dst, send_sem=ss, recv_sem=rs, device_id=device
        ).wait_recv()

    def dx_cols(at):
        return pl.ds(pl.multiple_of(DX * at, DX), DX)

    own_weight = pltpu.make_async_copy(ow_hbm.at[:, dx_cols(x)], wown, w_sem)
    own_weight.start()
    for pair in range(SEG // 2):
        spot = []
        for half in range(2):
            h = 2 * pair + half
            spot += [
                q_ref[:, HEAD * (2 * h + piece) : HEAD * (2 * h + piece + 1)].astype(F32)
                for piece in range(2)
            ]
        k = pair // 2
        row = HEAD * (k % 2) + 32 * (k // 2) + 16 * (pair % 2)
        qbuf[0, row : row + 16, :] = jnp.concatenate(spot, axis=0).astype(BF16)
    qbuf[WINDOW] = jnp.zeros((2 * ROWS, HEAD), BF16)
    greet()

    for c in range(2):
        rows = pl.ds(HEAD * c, HEAD)
        for slot in range(1, WINDOW):
            send(
                qbuf.at[0, rows],
                qbuf.at[slot, rows],
                q_ss.at[c, slot],
                q_rs.at[c, slot],
                {"seg": lax.rem(me - slot + SEG, SEG)},
            )

    early()

    closure_t = closure_transposed(par_ref[...])
    position_row = pos_ref[...]
    node_row = scored_nodes(node_ref[...], position_row)
    sub = iota((NODES, ROWS), 0)
    row_hot_t = hot(sub.astype(F32) == node_row)
    reach_t = mm(closure_t, row_hot_t).astype(BF16)
    own_nodes = node_ref[pl.ds(me, 1), :]
    token_hot = jnp.where(sub == own_nodes, 1.0, 0.0).T.astype(BF16)
    linked = mm(token_hot, reach_t)
    visible = hot((linked > 0.5) & (sub + TOK * me <= position_row))
    wide_sub = iota((ROWS, 2 * ROWS), 0)
    wide_lane = iota((ROWS, 2 * ROWS), 1)
    wanted = lax.rem(SCORE * (me + wide_lane // 32) + lax.rem(wide_lane, SCORE), ROWS)
    mask = mm(visible, hot((wide_sub == wanted) & (wide_lane < 32 * WINDOW))) > 0.5

    scale = HEAD ** (-0.5)
    for c in range(2):
        for slot in range(1, WINDOW):
            landed(
                qbuf.at[slot, pl.ds(HEAD * c, HEAD)],
                q_ss.at[c, slot],
                q_rs.at[c, slot],
                {"seg": lax.rem(me + slot, SEG)},
            )
        for i in range(4):
            k = 2 * i + c
            row = HEAD * c + 32 * i
            query = qbuf[:, row : row + 32, :].reshape(2 * ROWS, HEAD)
            lanes = slice(HEAD * k, HEAD * k + HEAD)
            scores = jnp.where(mask, mm_nt(k_ref[:, lanes], query) * scale, NEGATIVE)
            top = jnp.max(scores, axis=0, keepdims=True)
            power = jnp.where(mask, jnp.exp(scores - top), 0.0)
            raised[4 * c + i] = power
            parts[c, WINDOW - 1, i : i + 1, :] = top
            parts[c, WINDOW - 1, 4 + i : 5 + i, :] = jnp.sum(power, axis=0, keepdims=True)
        for delta in range(1, WINDOW):
            for way in (delta, -delta):
                slot = WINDOW - 1 - way
                send(
                    parts.at[c, WINDOW - 1],
                    parts.at[c, slot],
                    p_ss.at[c, slot],
                    p_rs.at[c, slot],
                    {"seg": lax.rem(me + way + SEG, SEG)},
                )

    core = lax.rem(grp, 2)
    level = grp // 2

    def slab_of(plane, height):
        return pl.ds(pl.multiple_of(32 * (Y * plane + height), 32), 32)

    slab = slab_of(core, level)
    for delta in range(1, X):
        send(
            ow_hbm.at[slab, dx_cols(lax.rem(x + delta, X))],
            wx.at[delta - 1, slab],
            wx_ss.at[delta - 1],
            wx_rs.at[delta - 1],
            at_x(delta),
        )
    part_slot = iota((4, 2 * ROWS), 1) // 32
    for c in range(2):
        tops = []
        totals = []
        for away in range(1 - WINDOW, WINDOW):
            slot = away + WINDOW - 1
            if away != 0:
                landed(
                    parts.at[c, slot],
                    p_ss.at[c, slot],
                    p_rs.at[c, slot],
                    {"seg": lax.rem(me + away + SEG, SEG)},
                )
            value = parts[c, slot]
            if away != 0:
                value = pltpu.roll(value, (32 * away) % (2 * ROWS), 1)
            valid = (part_slot >= away) & (part_slot < away + WINDOW)
            tops.append(jnp.where(valid, value[0:4], NEGATIVE))
            totals.append(jnp.where(valid, value[4:8], 0.0))
        peak = tops[0]
        for top in tops[1:]:
            peak = jnp.maximum(peak, top)
        whole = totals[0] * jnp.exp(tops[0] - peak)
        for top, total in zip(tops[1:], totals[1:]):
            whole = whole + total * jnp.exp(top - peak)
        own_top = parts[c, WINDOW - 1][0:4]
        factors[c, 0:4, :] = jnp.exp(own_top - peak) / jnp.where(whole > 0.0, whole, 1.0)
        for step in range(4):
            i = lax.rem(z // 2 + step, 4)
            at = 4 * c + i
            lanes = pl.ds(pl.multiple_of(HEAD * (2 * i + c), HEAD), HEAD)
            probs = raised[at] * factors[c, pl.ds(i, 1), :]
            mixed = mm(probs.T.astype(BF16), v_ref[:, lanes]).reshape(SLOTS, 4, 8, HEAD)
            for pair in range(4):
                osend[at, pair] = mixed[0:WINDOW, pair].reshape(8 * WINDOW, HEAD)
            for delta in (1, 3, 2):
                send(
                    osend.at[at, lax.rem(x + delta, X)],
                    oxr.at[at, delta - 1],
                    ox_ss.at[4 * c + step, delta - 1],
                    ox_rs.at[at, delta - 1],
                    at_x(delta),
                )

    for delta in range(1, X):
        landed(wx.at[delta - 1, slab], wx_ss.at[delta - 1], wx_rs.at[delta - 1], at_x(delta))
    for delta in range(1, Y):
        send(
            wx.at[:, slab],
            wx.at[:, slab],
            wy_ss.at[delta],
            wy_rs.at[level],
            {"grp": 2 * lax.rem(level + delta, Y) + core, "seg": me},
        )
    place_row = iota((16, 16), 0)
    place_col = iota((16, 16), 1)
    place = hot((place_row == SCORE * x + place_col) & (place_col < SCORE))
    for delta in range(X):
        cols = resid_ref[:, dx_cols(lax.rem(x + delta, X))]
        padded = jnp.concatenate([cols.astype(F32), jnp.zeros((16 - SCORE, DX), F32)], axis=0)
        rsend[delta] = mm(place, padded.astype(BF16)).astype(BF16)
        if delta:
            send(rsend.at[delta], rrecv.at[delta - 1], r_ss.at[delta], r_rs.at[delta], at_x(delta))

    guarded = []
    for c in range(2):
        for step in range(4):
            i = lax.rem(z // 2 + step, 4)
            at = 4 * c + i
            target = 2 * i + c
            for delta in (1, 3, 2):
                landed(
                    oxr.at[at, delta - 1],
                    ox_ss.at[4 * c + step, delta - 1],
                    ox_rs.at[at, delta - 1],
                    at_x(delta),
                )
            ozs[at] = jnp.zeros((8 * OWNERS, HEAD), F32)
            ozs[at, pl.ds(pl.multiple_of(8 * x, 8), 8 * WINDOW), :] = osend[at, x]
            for delta in range(1, X):
                span = pl.ds(pl.multiple_of(8 * lax.rem(x - delta + X, X), 8), 8 * WINDOW)
                ozs[at, span, :] = ozs[at, span, :] + oxr[at, delta - 1]
            away_copy = pltpu.make_async_remote_copy(
                src_ref=ozs.at[at],
                dst_ref=ozr.at[z],
                send_sem=oz_ss.at[4 * c + step],
                recv_sem=oz_rs.at[z],
                device_id={"seg": target * X + x},
            )
            if step == 0:
                guarded.append((target, away_copy))

                @pl.when(target == z)
                def _():
                    ozr[z] = ozs[at]

                @pl.when(target != z)
                def _():
                    away_copy.start()

            else:
                away_copy.start()
                pending.append(away_copy)

    middle(closure_t, row_hot_t)
    for delta in range(1, Y):
        other = lax.rem(level + delta, Y)
        landed(
            wx.at[:, slab_of(core, other)],
            wy_ss.at[delta],
            wy_rs.at[other],
            {"grp": 2 * other + core, "seg": me},
        )
    send(
        wx.at[:, pl.ds(pl.multiple_of(ROWS * core, ROWS), ROWS)],
        wx.at[:, pl.ds(pl.multiple_of(ROWS * core, ROWS), ROWS)],
        wy_ss.at[Y],
        wy_rs.at[Y],
        {"grp": 2 * level + 1 - core, "seg": me},
    )

    for delta in range(1, Z):
        source = lax.rem(z + delta, Z)
        landed(ozr.at[source], oz_ss.at[0], oz_rs.at[source], at_z(delta))
    sums = [None] * SEG
    for source in range(Z):
        block = ozr[source]
        for slot in range(OWNERS):
            row = X * source + slot
            if row < SEG:
                term = block[8 * slot : 8 * slot + 8]
                sums[row] = term if sums[row] is None else sums[row] + term
    stacked = jnp.concatenate(sums, axis=0).astype(BF16)
    out_row = iota((2 * ROWS, 2 * ROWS), 0)
    in_row = iota((2 * ROWS, 2 * ROWS), 1)
    packed = lax.rem(out_row, ROWS)
    from_row = 8 * (packed // SCORE) + SCORE * (out_row // ROWS) + lax.rem(packed, SCORE)
    sorted_rows = mm(hot(in_row == from_row), stacked).astype(BF16)
    left = jnp.concatenate([sorted_rows[0:ROWS], sorted_rows[ROWS : 2 * ROWS]], axis=1)
    mixs[...] = left
    for delta in (1, 3, 2):
        send(mixs, mixr.at[delta - 1], m_ss.at[delta - 1], m_rs.at[delta - 1], at_x(delta))
    own_weight.wait()
    product = mm(left, wown[...])
    landed(
        wx.at[:, pl.ds(pl.multiple_of(ROWS * (1 - core), ROWS), ROWS)],
        wy_ss.at[Y],
        wy_rs.at[Y],
        {"grp": 2 * level + 1 - core, "seg": me},
    )
    for delta in (1, 3, 2):
        landed(mixr.at[delta - 1], m_ss.at[delta - 1], m_rs.at[delta - 1], at_x(delta))
        product = product + mm(mixr[delta - 1], wx[delta - 1])
    zown[...] = product

    for delta in (1, 7, 2, 6, 3, 5, 4):
        target = lax.rem(z + delta, Z)
        zsend[delta] = encode(zown[pl.ds(pl.multiple_of(16 * target, 16), 16), :])
        send(zsend.at[delta], zrecv.at[delta], z_ss.at[delta], z_rs.at[delta], at_z(delta))
    hidden = zown[pl.ds(pl.multiple_of(16 * z, 16), 16), :] + rsend[0].astype(F32)
    for delta in range(1, X):
        landed(rrecv.at[delta - 1], r_ss.at[delta], r_rs.at[delta], at_x(delta))
        hidden = hidden + rrecv[delta - 1].astype(F32)
    for delta in (1, 7, 2, 6, 3, 5, 4):
        landed(zrecv.at[delta], z_ss.at[delta], z_rs.at[delta], at_z(delta))
        hidden = hidden + decode(zrecv[delta])
    squares = jnp.sum(hidden * hidden, axis=1, keepdims=True)
    sqs[...] = jnp.broadcast_to(squares, sqs.shape)
    for delta in (1, 3, 2):
        send(sqs, sqr.at[delta - 1], s_ss.at[delta - 1], s_rs.at[delta - 1], at_x(delta))
    gain = gain_ref[dx_cols(x)].astype(F32).reshape(1, DX)
    for delta in (1, 3, 2):
        landed(sqr.at[delta - 1], s_ss.at[delta - 1], s_rs.at[delta - 1], at_x(delta))
    power = (sqs[...] + sqr[0] + sqr[1] + sqr[2])[:, 0:1] / D
    normed = (hidden * lax.rsqrt(power + 1e-06) * gain).astype(BF16)

    def drain():
        for copy in pending:
            copy.wait_send()
        for target, copy in guarded:

            @pl.when(target != z)
            def _():
                copy.wait_send()

    return normed, drain


def front_scratch():
    sems = pltpu.SemaphoreType.DMA
    return [
        pltpu.VMEM((SLOTS, 2 * ROWS, HEAD), BF16),
        pltpu.VMEM((KV_HEADS, TOK, 2 * ROWS), F32),
        pltpu.VMEM((2, 2 * WINDOW - 1, 8, 2 * ROWS), F32),
        pltpu.VMEM((2, 8, 2 * ROWS), F32),
        pltpu.VMEM((KV_HEADS, X, 8 * WINDOW, HEAD), F32),
        pltpu.VMEM((KV_HEADS, X - 1, 8 * WINDOW, HEAD), F32),
        pltpu.VMEM((KV_HEADS, 8 * OWNERS, HEAD), F32),
        pltpu.VMEM((Z, 8 * OWNERS, HEAD), F32),
        pltpu.VMEM((ROWS, 2 * HEAD), BF16),
        pltpu.VMEM((X - 1, ROWS, 2 * HEAD), BF16),
        pltpu.VMEM((2 * HEAD, DX), BF16),
        pltpu.VMEM((X - 1, 2 * HEAD, DX), BF16),
        pltpu.VMEM((X, 16, DX), BF16),
        pltpu.VMEM((X - 1, 16, DX), BF16),
        pltpu.VMEM((Z, 16, DX + HEAD), jnp.int16),
        pltpu.VMEM((ROWS, DX), F32),
        pltpu.VMEM((Z, 16, DX + HEAD), jnp.int16),
        pltpu.VMEM((16, HEAD), F32),
        pltpu.VMEM((X - 1, 16, HEAD), F32),
        sems,
        sems((2, WINDOW)),
        sems((2, WINDOW)),
        sems((2, 2 * WINDOW - 1)),
        sems((2, 2 * WINDOW - 1)),
        sems((KV_HEADS, X - 1)),
        sems((KV_HEADS, X - 1)),
        sems((Z,)),
        sems((Z,)),
        sems((X - 1,)),
        sems((X - 1,)),
        sems((X - 1,)),
        sems((X - 1,)),
        sems((GRP,)),
        sems((GRP,)),
        sems((X,)),
        sems((X,)),
        sems((Z,)),
        sems((Z,)),
        sems((X - 1,)),
        sems((X - 1,)),
    ]


def encode(value):
    most = jnp.maximum(jnp.max(jnp.abs(value), axis=1, keepdims=True), 1e-30)
    level = jnp.ceil(jnp.log2(most * (1.0 / 32000.0)))
    scaled = jnp.round(value * jnp.exp2(-level)).astype(jnp.int32)
    levels = jnp.broadcast_to(level.astype(jnp.int32), (value.shape[0], HEAD))
    return jnp.concatenate([scaled, levels], axis=1).astype(jnp.int16)


def decode(code):
    wide = code.astype(jnp.int32).astype(F32)
    return wide[:, 0:DX] * jnp.exp2(wide[:, DX : DX + 1])


def vmem():
    return pl.BlockSpec(memory_space=pltpu.VMEM)


SIZE = {"x": X, "y": Y, "z": Z}


def plan_gather():
    messages = []
    by_key = {}
    for part, (offset, width, order) in enumerate(PARTS):
        for stage, axis in enumerate(order):
            count = SIZE[axis]
            chunked = stage == 2
            inner = range(SIZE[order[1]]) if chunked else (None,)
            amount = 32 * width
            for name in order[:stage]:
                amount *= SIZE[name]
            if chunked:
                amount //= SIZE[order[1]]
            for step in range(1, count // 2 + 1):
                for rank, chunk in enumerate(inner):
                    for way in (1, -1):
                        half = None
                        if step == count // 2:
                            if chunked:
                                if (way > 0) != (rank % 2 == 0):
                                    continue
                            elif stage == 0:
                                if way < 0:
                                    continue
                            else:
                                half = 0 if way > 0 else 1
                        key = (part, stage, step, chunk, way)
                        by_key[key] = len(messages)
                        messages.append(
                            dict(
                                part=part, stage=stage, axis=axis, step=step, chunk=chunk, way=way, half=half,
                                size=amount if half is None else amount // 2,
                            )
                        )

    def bringing(part, stage, offset):
        count = SIZE[PARTS[part][2][stage]]
        offset %= count
        if offset == 0:
            return []
        found = []
        for key, index in by_key.items():
            if key[0] == part and key[1] == stage and (-key[4] * key[2]) % count == offset:
                found.append(index)
        return found

    def whole_stage(part, stage):
        return [index for key, index in by_key.items() if key[0] == part and key[1] == stage]

    for message in messages:
        part, stage = message["part"], message["stage"]
        if message["step"] > 1:
            if message["chunk"] is None:
                needs = bringing(part, stage, -message["way"] * (message["step"] - 1))
            else:
                needs = [by_key[part, stage, message["step"] - 1, message["chunk"], message["way"]]]
        elif stage == 0:
            needs = []
        elif stage == 1:
            needs = whole_stage(part, 0)
        elif message["chunk"] == 0:
            needs = whole_stage(part, 0)
        else:
            needs = bringing(part, 1, message["chunk"])
        message["needs"] = needs
    tasks = []
    for part, (offset, width, order) in enumerate(PARTS):
        count = SIZE[order[2]]
        groups = [(0,)] + [(step, -step) for step in range(1, count // 2)] + [(count // 2,)]
        if part == 1:
            groups = [(item,) for group in groups for item in group]
        for group in groups:
            needs = []
            for item in group:
                if item == 0:
                    needs += whole_stage(part, 0) + whole_stage(part, 1)
                else:
                    needs += bringing(part, 2, item)
            tasks.append(dict(part=part, group=group, needs=needs))

    free = {}
    ready = {}
    arrive = {}
    left = set(range(len(messages)))
    while left:
        best = None
        for index in sorted(left):
            message = messages[index]
            if all(need in arrive for need in message["needs"]):
                at = max([arrive[need] for need in message["needs"]], default=0.0)
                link = (message["axis"], message["way"])
                begin = max(at, free.get(link, 0.0))
                if best is None or (begin, at, index) < best[0]:
                    best = ((begin, at, index), index, link, at)
        (begin, at, unused), index, link, at = best
        left.remove(index)
        finish = begin + messages[index]["size"] / 46e3
        free[link] = finish
        ready[index] = at
        arrive[index] = finish + 0.9
    events = [(ready[index], 0, index) for index in ready]
    events += [
        (max(arrive[need] for need in task["needs"]) + 0.2, 1, number) for number, task in enumerate(tasks)
    ]
    return messages, tasks, sorted(events)


GATHERS = len(plan_gather()[0])


def merge_tiles(tiles):
    peak = tiles[0]
    for tile in tiles[1:]:
        peak = jnp.maximum(peak, tile)
    raised = jnp.exp(tiles[0] - peak)
    added = tiles[0]
    for tile in tiles[1:]:
        raised = raised + jnp.exp(tile - peak)
        added = added + tile
    return jnp.where(iota(peak.shape, 0) == 0, peak + jnp.log(raised), added)


def program_body(
    q_hbm, k_hbm, v_hbm, node_hbm, par_hbm, pos_hbm, ow_hbm, resid_hbm, gain_ref,
    w_hbm, leaf_hbm, target_hbm, old_hbm, adv_hbm,
    answer_ref,
    q_ref, k_ref, v_ref, node_ref, par_ref, pos_ref, resid_ref, leaf_ref, target_ref, old_ref, adv_ref,
    in_sems, *rest,
):
    front_count = len(front_scratch())
    front_refs = rest[:front_count]
    (
        w, part_a, part_b, part_c, logits, paths, tiny, info, info_x, info_z, info_y,
        stat_s, stat_y, stat_z, mine_x, last_s, last_r,
        w_sem, w_ss, w_rs, g_ss, g_rs, i_ss, i_rs, t_ss, t_rs, y_ss, y_rs, l_ss, l_rs,
    ) = rest[front_count:]
    grp = lax.axis_index("grp")
    me = lax.axis_index("seg")
    y = grp // 2
    core = lax.rem(grp, 2)
    z = me // X
    x = lax.rem(me, X)
    at = {"x": x, "y": y, "z": z}
    size = {"x": X, "y": Y, "z": Z}

    def peer(axis, delta):
        moved = dict(at)
        moved[axis] = lax.rem(at[axis] + delta + size[axis], size[axis])
        return {"grp": moved["y"] * 2 + core, "seg": moved["z"] * X + moved["x"]}

    barrier = pltpu.get_barrier_semaphore()
    offsets = [way * delta for delta in range(1, WINDOW) for way in (1, -1)]
    offsets += [delta for delta in range(X, SEG, X) if min(delta, SEG - delta) >= WINDOW]
    partners = [{"seg": lax.rem(me + delta + SEG, SEG)} for delta in offsets]
    partners += [{"grp": lax.rem(grp + delta, GRP), "seg": me} for delta in range(1, GRP)]
    partners += [
        {"grp": lax.rem(y + dy, Y) * 2 + core, "seg": z * X + lax.rem(x + dx, X)}
        for dy in range(1, Y)
        for dx in range(1, X)
    ]
    for partner in partners:
        pl.semaphore_signal(barrier, 1, device_id=partner)
    loads = []
    for index, (src, dst) in enumerate(
        (
            (q_hbm, q_ref), (k_hbm, k_ref), (v_hbm, v_ref), (node_hbm, node_ref), (par_hbm, par_ref),
            (pos_hbm, pos_ref), (resid_hbm, resid_ref), (leaf_hbm, leaf_ref),
            (target_hbm, target_ref), (old_hbm, old_ref), (adv_hbm, adv_ref),
        )
    ):
        copy = pltpu.make_async_copy(src, dst, in_sems.at[index])
        copy.start()
        loads.append(copy)
    own_w = pltpu.make_async_copy(w_hbm, w.at[:, 0:VOC], w_sem)
    loads[0].wait()

    tile_sub = iota((8, ROWS), 0)
    tile_lane = iota((8, ROWS), 1)
    pending = []
    swap = pltpu.make_async_remote_copy(
        src_ref=w_hbm,
        dst_ref=w.at[:, VOC : 2 * VOC],
        send_sem=w_ss,
        recv_sem=w_rs,
        device_id={"grp": y * 2 + 1 - core, "seg": me},
    )

    def spread(axis, sources, into, base, ss, rs):
        count = size[axis]
        here = at[axis]
        for delta in range(1, count):
            there = lax.rem(here + delta, count)
            copy = pltpu.make_async_remote_copy(
                src_ref=sources(there),
                dst_ref=into.at[here],
                send_sem=ss.at[base + delta],
                recv_sem=rs.at[base + here],
                device_id=peer(axis, delta),
            )
            copy.start()
            pending.append(copy)

    def collect(axis, into, base, ss, rs):
        count = size[axis]
        here = at[axis]
        for delta in range(1, count):
            there = lax.rem(here + delta, count)
            pltpu.make_async_remote_copy(
                src_ref=into.at[there],
                dst_ref=into.at[there],
                send_sem=ss.at[base + delta],
                recv_sem=rs.at[base + there],
                device_id=peer(axis, delta),
            ).wait_recv()

    bufs = (part_a, part_b, part_c)
    messages, tasks, events = plan_gather()

    def block(message, moved):
        axis, stage = message["axis"], message["stage"]
        order = PARTS[message["part"]][2]
        where = []
        for name in "xyz":
            if name == axis:
                where.append(lax.rem(at[name] + moved + 2 * size[name], size[name]))
            elif name not in order[:stage]:
                where.append(at[name])
            elif message["chunk"] is not None and name == order[1]:
                where.append(lax.rem(at[name] + message["chunk"], size[name]))
            elif message["half"] is not None and name == order[0]:
                cut = size[name] // 2
                where.append(pl.ds(message["half"] * cut, cut))
            else:
                where.append(slice(None))
        return bufs[message["part"]].at[tuple(where)]

    def ring(index, moved):
        message = messages[index]
        ref = block(message, moved)
        return pltpu.make_async_remote_copy(
            src_ref=ref,
            dst_ref=ref,
            send_sem=g_ss.at[index],
            recv_sem=g_rs.at[index],
            device_id=peer(message["axis"], message["way"]),
        )

    def head_task(task):
        part = task["part"]
        offset, width, order = PARTS[part]
        buf = bufs[part]
        axis = order[2]

        def columns(n, carry):
            cols = pl.ds(pl.multiple_of(256 * n, 256), 256)
            if axis == "x":
                here = lax.rem(x + task["group"][0] + X, X)
                rows = buf[here].reshape(Y * Z * 16, width)
                weight = w[pl.ds(pl.multiple_of(DX * here + offset, 128), width), cols]
                logits[:, :, :, cols] = logits[:, :, :, cols] + mm(rows, weight).reshape(Y, Z, 16, 256)
                return carry
            places = [lax.rem(at[axis] + item + size[axis], size[axis]) for item in task["group"]]
            total = None
            for index in range(X):
                if axis == "z":
                    rows = [buf[index, :, place].reshape(Y * 16, width) for place in places]
                else:
                    rows = [buf[index, place].reshape(Z * 16, width) for place in places]
                rows = rows[0] if len(rows) == 1 else jnp.concatenate(rows, axis=0)
                term = mm(rows, w[DX * index + offset : DX * index + offset + width, cols])
                total = term if total is None else total + term
            high = total.shape[0] // len(places)
            for number, place in enumerate(places):
                piece = total[high * number : high * number + high]
                if axis == "z":
                    logits[:, place, :, cols] = logits[:, place, :, cols] + piece.reshape(Y, 16, 256)
                else:
                    logits[place, :, :, cols] = logits[place, :, :, cols] + piece.reshape(Z, 16, 256)
            return carry

        lax.fori_loop(0, 2 * VOC // 256, columns, 0)

    def tell():
        tiny[...] = jnp.zeros_like(tiny)
        tiny[0:1, 0:SCORE] = target_ref[...].astype(F32)
        tiny[1:2, 0:SCORE] = old_ref[...]
        tiny[2:3, 0:2] = adv_ref[...]
        start = tiny[...]
        info[...] = jnp.where(
            tile_sub < 2, pltpu.roll(start, SCORE * me, 1), pltpu.roll(start, 2 * me, 1)
        )
        info_x[x] = info[...]
        spread("x", lambda there: info_x.at[x], info_x, 0, i_ss, i_rs)
        yield
        collect("x", info_x, 0, i_ss, i_rs)
        info_z[z] = info_x[0] + info_x[1] + info_x[2] + info_x[3]
        spread("z", lambda there: info_z.at[z], info_z, X, i_ss, i_rs)
        yield
        collect("z", info_z, X, i_ss, i_rs)
        whole = info_z[0]
        for index in range(1, Z):
            whole = whole + info_z[index]
        info_y[y] = whole
        spread("y", lambda there: info_y.at[y], info_y, X + Z, i_ss, i_rs)
        yield
        collect("y", info_y, X + Z, i_ss, i_rs)

    talk = tell()

    def greet():
        pl.semaphore_wait(barrier, len(partners))

    def early():
        own_w.start()
        swap.start()
        for copy in loads[1:]:
            copy.wait()
        next(talk)

    def middle(closure_t, row_hot_t):
        next(talk)
        logits[...] = jnp.zeros_like(logits)
        leaf_hot_t = hot(iota((NODES, LEAVES), 0) == leaf_ref[...])
        leaf_reach_t = mm(closure_t, leaf_hot_t)
        filler = jnp.zeros((NODES, NODES - LEAVES), F32)
        leaf_reach = jnp.concatenate([leaf_reach_t, filler], axis=1).T
        paths[...] = mm(leaf_reach.astype(BF16), row_hot_t)

    normed, drain = front(
        me, grp, q_ref, k_ref, v_ref, node_ref, par_ref, pos_ref, ow_hbm, resid_ref, gain_ref,
        *front_refs, greet, early, middle,
    )
    for (offset, width, order), buf in zip(PARTS, bufs):
        buf[x, y, z] = normed[:, offset : offset + width]
    next(talk)
    seen = set()

    def await_all(needs):
        for index in needs:
            if index not in seen:
                seen.add(index)
                ring(index, -messages[index]["way"] * messages[index]["step"]).wait_recv()

    loaded = False
    for unused, kind, index in events:
        if kind == 0:
            await_all(messages[index]["needs"])
            copy = ring(index, -messages[index]["way"] * (messages[index]["step"] - 1))
            copy.start()
            pending.append(copy)
        else:
            if not loaded:
                own_w.wait()
                swap.wait_recv()
                loaded = True
            await_all(tasks[index]["needs"])
            head_task(tasks[index])
    for rest_of in talk:
        pass

    voc_lane = iota((ROWS, 2 * VOC), 1)
    own_base = (grp * SEG + me) * VOC
    other_base = ((2 * y + 1 - core) * SEG + me) * VOC - VOC
    voc_id = (voc_lane + jnp.where(voc_lane < VOC, own_base, other_base)).astype(F32)
    targets = jnp.concatenate(
        [info_y[...].reshape(8 * Y, ROWS), jnp.zeros((ROWS - 8 * Y, ROWS), F32)], axis=0
    ).T
    square_lane = iota((ROWS, ROWS), 1)
    for index in range(Y):
        block = logits[index].reshape(ROWS, 2 * VOC)
        top = jnp.max(block, axis=1, keepdims=True)
        lse = top + jnp.log(jnp.sum(jnp.exp(block - top), axis=1, keepdims=True))
        found = voc_id == targets[:, 8 * index : 8 * index + 1]
        picked = jnp.sum(jnp.where(found, block, 0.0), axis=1, keepdims=True)
        both = jnp.where(square_lane == 0, lse, jnp.where(square_lane == 1, picked, 0.0))
        stat_s[index] = both.T[0:8]
    def square(dy, dx):
        ty = lax.rem(y + dy, Y)
        tx = lax.rem(x + dx, X)
        device = {"grp": ty * 2 + core, "seg": z * X + tx}
        return ty, tx, device

    steps = [(dy, dx) for dy in range(Y) for dx in range(X) if dy or dx]
    for dy, dx in steps:
        ty, tx, device = square(dy, dx)
        copy = pltpu.make_async_remote_copy(
            src_ref=stat_s.at[ty],
            dst_ref=stat_y.at[y * X + x],
            send_sem=y_ss.at[dy * X + dx],
            recv_sem=y_rs.at[y * X + x],
            device_id=device,
        )
        copy.start()
        pending.append(copy)
    stat_y[y * X + x] = stat_s[y]

    path = paths[...]
    counts = jnp.maximum(jnp.sum(path, axis=1, keepdims=True), 1.0)
    for dy, dx in steps:
        ty, tx, device = square(dy, dx)
        pltpu.make_async_remote_copy(
            src_ref=stat_s.at[ty],
            dst_ref=stat_y.at[ty * X + tx],
            send_sem=y_ss.at[dy * X + dx],
            recv_sem=y_rs.at[ty * X + tx],
            device_id=device,
        ).wait_recv()
    mine_x[...] = merge_tiles([stat_y[index] for index in range(X * Y)])
    spread("z", lambda there: mine_x, stat_z, Y + X, t_ss, t_rs)
    stat_z[z] = mine_x[...]
    collect("z", stat_z, Y + X, t_ss, t_rs)
    merged = merge_tiles([stat_z[index] for index in range(Z)])

    own_info = info_y[y]
    token_row = merged[1:2] - merged[0:1] - own_info[1:2]
    shift = lax.rem(ROWS - SCORE * me, ROWS)
    answer_ref[0:1, :] = pltpu.roll(jnp.broadcast_to(token_row, (8, ROWS)), shift, 1)[0:1]
    means = jnp.sum(path * token_row, axis=1, keepdims=True) / counts
    leaf_row = jnp.broadcast_to(means, (ROWS, ROWS)).T[0:8]
    answer_ref[1:2, :] = pltpu.roll(leaf_row, lax.rem(ROWS - 2 * me, ROWS), 1)[0:1]
    gains = own_info[2:3]
    ratio = jnp.exp(leaf_row)
    terms = jnp.minimum(ratio * gains, jnp.clip(ratio, 1.0 - EPS_LOW, 1.0 + EPS_HIGH) * gains)
    terms = jnp.where((tile_sub == 0) & (tile_lane < LEAVES), terms, 0.0)
    last_s[...] = terms

    last = []
    for delta in range(1, GRP):
        copy = pltpu.make_async_remote_copy(
            src_ref=last_s,
            dst_ref=last_r.at[grp],
            send_sem=l_ss.at[delta],
            recv_sem=l_rs.at[grp],
            device_id={"grp": lax.rem(grp + delta, GRP), "seg": me},
        )
        copy.start()
        last.append(copy)
    last_r[grp] = terms
    for delta in range(1, GRP):
        there = lax.rem(grp + delta, GRP)
        pltpu.make_async_remote_copy(
            src_ref=last_s,
            dst_ref=last_r.at[there],
            send_sem=l_ss.at[delta],
            recv_sem=l_rs.at[there],
            device_id={"grp": there, "seg": me},
        ).wait_recv()
    everything = last_r[0]
    for index in range(1, GRP):
        everything = everything + last_r[index]
    total = -jnp.sum(everything, axis=(0, 1), keepdims=True) / (LEAVES * GRP)
    answer_ref[2:8, :] = jnp.broadcast_to(total, (6, ROWS))

    drain()
    for copy in pending:
        copy.wait_send()
    swap.wait_send()
    for copy in last:
        copy.wait_send()


def split_body(answer_ref, token_ref, leaf_ref, loss_ref):
    token_ref[...] = answer_ref[0:1, 0:SCORE]
    leaf_ref[...] = answer_ref[1:2, 0:2]
    loss_ref[...] = answer_ref[2:3, 0:1]


def body(
    queries, keys, values, node_ids, parents, score_pos, out_weight, resid, norm_gain,
    vocab_weight, targets, old_logp, leaf_node, advantages,
):
    sems = pltpu.SemaphoreType.DMA
    tile = pltpu.VMEM((8, ROWS), F32)

    def tiles(count):
        return pltpu.VMEM((count, 8, ROWS), F32)

    anywhere = pl.BlockSpec(memory_space=pl.ANY)
    answer = pl.pallas_call(
        program_body,
        out_shape=jax.ShapeDtypeStruct((8, ROWS), F32),
        in_specs=[anywhere] * 8 + [vmem()] + [anywhere] * 5,
        out_specs=vmem(),
        scratch_shapes=[
            pltpu.VMEM((SCORE, 64 * HEAD), BF16),
            pltpu.VMEM((TOK, KV_HEADS * HEAD), BF16),
            pltpu.VMEM((TOK, KV_HEADS * HEAD), BF16),
            pltpu.VMEM((SEG, TOK), jnp.int32),
            pltpu.VMEM((1, NODES), jnp.int32),
            pltpu.VMEM((1, ROWS), jnp.int32),
            pltpu.VMEM((SCORE, D), BF16),
            pltpu.VMEM((1, LEAVES), jnp.int32),
            pltpu.VMEM((1, SCORE), jnp.int32),
            pltpu.VMEM((1, SCORE), F32),
            pltpu.VMEM((1, 2), F32),
            sems((11,)),
        ]
        + front_scratch()
        + [pltpu.VMEM((D, 2 * VOC), BF16)]
        + [pltpu.VMEM((X, Y, Z, 16, width), BF16) for offset, width, order in PARTS]
        + [
            pltpu.VMEM((Y, Z, 16, 2 * VOC), F32),
            pltpu.VMEM((NODES, ROWS), F32),
            tile,
            tile,
            tiles(X),
            tiles(Z),
            tiles(Y),
            tiles(Y),
            tiles(X * Y),
            tiles(Z),
            tile,
            tile,
            tiles(GRP),
            sems,
            sems,
            sems,
            sems((GATHERS,)),
            sems((GATHERS,)),
            sems((X + Y + Z,)),
            sems((X + Y + Z,)),
            sems((X + Y + Z,)),
            sems((X + Y + Z,)),
            sems((X * Y,)),
            sems((X * Y,)),
            sems((GRP,)),
            sems((GRP,)),
        ],
        compiler_params=pltpu.CompilerParams(
            collective_id=0, has_side_effects=True, vmem_limit_bytes=58 * MIB
        ),
    )(
        queries[0], keys[0], values[0], node_ids.reshape(SEG, TOK), parents, score_pos, out_weight,
        resid[0], norm_gain, vocab_weight, leaf_node, targets, old_logp, advantages,
    )
    token, leaf, loss = pl.pallas_call(
        split_body,
        out_shape=(
            jax.ShapeDtypeStruct((1, SCORE), F32),
            jax.ShapeDtypeStruct((1, 2), F32),
            jax.ShapeDtypeStruct((1, 1), F32),
        ),
        in_specs=[vmem()],
        out_specs=(vmem(), vmem(), vmem()),
    )(answer)
    return (token, leaf, loss.reshape(()))


def solution(mesh):
    placed = (
        P("grp", "seg", None),
        P("grp", "seg", None),
        P("grp", "seg", None),
        P("grp", None),
        P("grp", None),
        P("grp", None),
        P("seg", None),
        P("grp", "seg", None),
        P(),
        P(None, ("grp", "seg")),
        P("grp", "seg"),
        P("grp", "seg"),
        P("grp", None),
        P("grp", "seg"),
    )
    return jax.shard_map(
        body,
        mesh=mesh,
        in_specs=placed,
        out_specs=(P("grp", "seg"), P("grp", "seg"), P()),
        check_vma=False,
    )
```

```python
import jax
import jax.numpy as jnp
from jax import lax
from jax.experimental import pallas as pl
from jax.experimental.pallas import tpu as pltpu
from jax.sharding import PartitionSpec as P

F32 = jnp.float32
BF16 = jnp.bfloat16
EPS_LOW = 0.0003
EPS_HIGH = 0.0004
NEGATIVE = -1e30
HEAD = 128
KV_HEADS = 8
X, Y, Z = 4, 4, 8
SEG = X * Z
GRP = 2 * Y
TOK = 128
ROWS = 128
NODES = 128
LEAVES = 64
SCORE = 4
WINDOW = 7
SLOTS = 8
OWNERS = X - 1 + WINDOW
D = 5120
DX = D // X
VOC = 384
PARTS = ((0, 384, "yxz"), (384, 512, "yzx"), (896, 384, "zxy"))
MIB = 1024 * 1024


def iota(shape, dim):
    return lax.broadcasted_iota(jnp.int32, shape, dim)


def hot(mask):
    return mask.astype(F32).astype(BF16)


def mm(a, b):
    return jnp.dot(a, b, preferred_element_type=F32)


def mm_nt(a, b):
    return lax.dot_general(a, b, (((1,), (1,)), ((), ())), preferred_element_type=F32)


def closure_transposed(parent_row):
    sub = iota((NODES, NODES), 0)
    lane = iota((NODES, NODES), 1)
    step = jnp.where((sub == parent_row) | (sub == lane), 1.0, 0.0)
    for squaring in range(3):
        half = step.astype(BF16)
        step = jnp.minimum(mm(half, half), 1.0)
    return step.astype(BF16)


def scored_nodes(node_table, position_row):
    table = jnp.concatenate([node_table.astype(F32), jnp.zeros((TOK - SEG, TOK), F32)], axis=0)
    across = table.T.astype(BF16)
    sub = iota((TOK, ROWS), 0)
    lane = iota((TOK, ROWS), 1)
    spread = mm(across, hot(sub == lane // SCORE))
    match = sub == position_row - TOK * (lane // SCORE)
    return jnp.sum(jnp.where(match, spread, 0.0), axis=0, keepdims=True)


def front(
    me, grp, q_ref, k_ref, v_ref, node_ref, par_ref, pos_ref, ow_hbm, resid_ref, gain_ref,
    qbuf, raised, parts, factors, osend, oxr, ozs, ozr, mixs, mixr, wown, wx, rsend, rrecv,
    zsend, zown, zrecv, sqs, sqr,
    w_sem, q_ss, q_rs, p_ss, p_rs, ox_ss, ox_rs, oz_ss, oz_rs, m_ss, m_rs, wx_ss, wx_rs, wy_ss, wy_rs,
    r_ss, r_rs, z_ss, z_rs, s_ss, s_rs, greet, early, middle,
):
    z = me // X
    x = lax.rem(me, X)
    pending = []

    def at_x(delta):
        return {"seg": z * X + lax.rem(x + delta, X)}

    def at_z(delta):
        return {"seg": lax.rem(z + delta, Z) * X + x}

    def send(src, dst, ss, rs, device):
        copy = pltpu.make_async_remote_copy(
            src_ref=src, dst_ref=dst, send_sem=ss, recv_sem=rs, device_id=device
        )
        copy.start()
        pending.append(copy)

    def landed(dst, ss, rs, device):
        pltpu.make_async_remote_copy(
            src_ref=dst, dst_ref=dst, send_sem=ss, recv_sem=rs, device_id=device
        ).wait_recv()

    def dx_cols(at):
        return pl.ds(pl.multiple_of(DX * at, DX), DX)

    own_weight = pltpu.make_async_copy(ow_hbm.at[:, dx_cols(x)], wown, w_sem)
    own_weight.start()
    for pair in range(SEG // 2):
        spot = []
        for half in range(2):
            h = 2 * pair + half
            spot += [
                q_ref[:, HEAD * (2 * h + piece) : HEAD * (2 * h + piece + 1)].astype(F32)
                for piece in range(2)
            ]
        k = pair // 2
        row = HEAD * (k % 2) + 32 * (k // 2) + 16 * (pair % 2)
        qbuf[0, row : row + 16, :] = jnp.concatenate(spot, axis=0).astype(BF16)
    qbuf[WINDOW] = jnp.zeros((2 * ROWS, HEAD), BF16)
    greet()

    for c in range(2):
        rows = pl.ds(HEAD * c, HEAD)
        for slot in range(1, WINDOW):
            send(
                qbuf.at[0, rows],
                qbuf.at[slot, rows],
                q_ss.at[c, slot],
                q_rs.at[c, slot],
                {"seg": lax.rem(me - slot + SEG, SEG)},
            )

    early()

    closure_t = closure_transposed(par_ref[...])
    position_row = pos_ref[...]
    node_row = scored_nodes(node_ref[...], position_row)
    sub = iota((NODES, ROWS), 0)
    row_hot_t = hot(sub.astype(F32) == node_row)
    reach_t = mm(closure_t, row_hot_t).astype(BF16)
    own_nodes = node_ref[pl.ds(me, 1), :]
    token_hot = jnp.where(sub == own_nodes, 1.0, 0.0).T.astype(BF16)
    linked = mm(token_hot, reach_t)
    visible = hot((linked > 0.5) & (sub + TOK * me <= position_row))
    wide_sub = iota((ROWS, 2 * ROWS), 0)
    wide_lane = iota((ROWS, 2 * ROWS), 1)
    wanted = lax.rem(SCORE * (me + wide_lane // 32) + lax.rem(wide_lane, SCORE), ROWS)
    mask = mm(visible, hot((wide_sub == wanted) & (wide_lane < 32 * WINDOW))) > 0.5

    scale = HEAD ** (-0.5)
    for c in range(2):
        for slot in range(1, WINDOW):
            landed(
                qbuf.at[slot, pl.ds(HEAD * c, HEAD)],
                q_ss.at[c, slot],
                q_rs.at[c, slot],
                {"seg": lax.rem(me + slot, SEG)},
            )
        for i in range(4):
            k = 2 * i + c
            row = HEAD * c + 32 * i
            query = qbuf[:, row : row + 32, :].reshape(2 * ROWS, HEAD)
            lanes = slice(HEAD * k, HEAD * k + HEAD)
            scores = jnp.where(mask, mm_nt(k_ref[:, lanes], query) * scale, NEGATIVE)
            top = jnp.max(scores, axis=0, keepdims=True)
            power = jnp.where(mask, jnp.exp(scores - top), 0.0)
            raised[4 * c + i] = power
            parts[c, WINDOW - 1, i : i + 1, :] = top
            parts[c, WINDOW - 1, 4 + i : 5 + i, :] = jnp.sum(power, axis=0, keepdims=True)
        for delta in range(1, WINDOW):
            for way in (delta, -delta):
                slot = WINDOW - 1 - way
                send(
                    parts.at[c, WINDOW - 1],
                    parts.at[c, slot],
                    p_ss.at[c, slot],
                    p_rs.at[c, slot],
                    {"seg": lax.rem(me + way + SEG, SEG)},
                )

    core = lax.rem(grp, 2)
    level = grp // 2

    def slab_of(plane, height):
        return pl.ds(pl.multiple_of(32 * (Y * plane + height), 32), 32)

    slab = slab_of(core, level)
    for delta in range(1, X):
        send(
            ow_hbm.at[slab, dx_cols(lax.rem(x + delta, X))],
            wx.at[delta - 1, slab],
            wx_ss.at[delta - 1],
            wx_rs.at[delta - 1],
            at_x(delta),
        )
    part_slot = iota((4, 2 * ROWS), 1) // 32
    for c in range(2):
        tops = []
        totals = []
        for away in range(1 - WINDOW, WINDOW):
            slot = away + WINDOW - 1
            if away != 0:
                landed(
                    parts.at[c, slot],
                    p_ss.at[c, slot],
                    p_rs.at[c, slot],
                    {"seg": lax.rem(me + away + SEG, SEG)},
                )
            value = parts[c, slot]
            if away != 0:
                value = pltpu.roll(value, (32 * away) % (2 * ROWS), 1)
            valid = (part_slot >= away) & (part_slot < away + WINDOW)
            tops.append(jnp.where(valid, value[0:4], NEGATIVE))
            totals.append(jnp.where(valid, value[4:8], 0.0))
        peak = tops[0]
        for top in tops[1:]:
            peak = jnp.maximum(peak, top)
        whole = totals[0] * jnp.exp(tops[0] - peak)
        for top, total in zip(tops[1:], totals[1:]):
            whole = whole + total * jnp.exp(top - peak)
        own_top = parts[c, WINDOW - 1][0:4]
        factors[c, 0:4, :] = jnp.exp(own_top - peak) / jnp.where(whole > 0.0, whole, 1.0)
        for step in range(4):
            i = lax.rem(z // 2 + step, 4)
            at = 4 * c + i
            lanes = pl.ds(pl.multiple_of(HEAD * (2 * i + c), HEAD), HEAD)
            probs = raised[at] * factors[c, pl.ds(i, 1), :]
            mixed = mm(probs.T.astype(BF16), v_ref[:, lanes]).reshape(SLOTS, 4, 8, HEAD)
            for pair in range(4):
                osend[at, pair] = mixed[0:WINDOW, pair].reshape(8 * WINDOW, HEAD)
            for delta in (2, 1, 3):
                send(
                    osend.at[at, lax.rem(x + delta, X)],
                    oxr.at[at, delta - 1],
                    ox_ss.at[4 * c + step, delta - 1],
                    ox_rs.at[at, delta - 1],
                    at_x(delta),
                )

    for delta in range(1, X):
        landed(wx.at[delta - 1, slab], wx_ss.at[delta - 1], wx_rs.at[delta - 1], at_x(delta))
    for delta in range(1, Y):
        send(
            wx.at[:, slab],
            wx.at[:, slab],
            wy_ss.at[delta],
            wy_rs.at[level],
            {"grp": 2 * lax.rem(level + delta, Y) + core, "seg": me},
        )
    place_row = iota((16, 16), 0)
    place_col = iota((16, 16), 1)
    place = hot((place_row == SCORE * x + place_col) & (place_col < SCORE))
    for delta in range(X):
        cols = resid_ref[:, dx_cols(lax.rem(x + delta, X))]
        padded = jnp.concatenate([cols.astype(F32), jnp.zeros((16 - SCORE, DX), F32)], axis=0)
        rsend[delta] = mm(place, padded.astype(BF16)).astype(BF16)
        if delta:
            send(rsend.at[delta], rrecv.at[delta - 1], r_ss.at[delta], r_rs.at[delta], at_x(delta))

    guarded = []
    for c in range(2):
        for step in range(4):
            i = lax.rem(z // 2 + step, 4)
            at = 4 * c + i
            target = 2 * i + c
            for delta in (1, 3, 2):
                landed(
                    oxr.at[at, delta - 1],
                    ox_ss.at[4 * c + step, delta - 1],
                    ox_rs.at[at, delta - 1],
                    at_x(delta),
                )
            ozs[at] = jnp.zeros((8 * OWNERS, HEAD), F32)
            ozs[at, pl.ds(pl.multiple_of(8 * x, 8), 8 * WINDOW), :] = osend[at, x]
            for delta in range(1, X):
                span = pl.ds(pl.multiple_of(8 * lax.rem(x - delta + X, X), 8), 8 * WINDOW)
                ozs[at, span, :] = ozs[at, span, :] + oxr[at, delta - 1]
            away_copy = pltpu.make_async_remote_copy(
                src_ref=ozs.at[at],
                dst_ref=ozr.at[z],
                send_sem=oz_ss.at[4 * c + step],
                recv_sem=oz_rs.at[z],
                device_id={"seg": target * X + x},
            )
            if step == 0:
                guarded.append((target, away_copy))

                @pl.when(target == z)
                def _():
                    ozr[z] = ozs[at]

                @pl.when(target != z)
                def _():
                    away_copy.start()

            else:
                away_copy.start()
                pending.append(away_copy)

    middle(closure_t, row_hot_t)
    for delta in range(1, Y):
        other = lax.rem(level + delta, Y)
        landed(
            wx.at[:, slab_of(core, other)],
            wy_ss.at[delta],
            wy_rs.at[other],
            {"grp": 2 * other + core, "seg": me},
        )
    send(
        wx.at[:, pl.ds(pl.multiple_of(ROWS * core, ROWS), ROWS)],
        wx.at[:, pl.ds(pl.multiple_of(ROWS * core, ROWS), ROWS)],
        wy_ss.at[Y],
        wy_rs.at[Y],
        {"grp": 2 * level + 1 - core, "seg": me},
    )

    for delta in range(1, Z):
        source = lax.rem(z + delta, Z)
        landed(ozr.at[source], oz_ss.at[0], oz_rs.at[source], at_z(delta))
    sums = [None] * SEG
    for source in range(Z):
        block = ozr[source]
        for slot in range(OWNERS):
            row = X * source + slot
            if row < SEG:
                term = block[8 * slot : 8 * slot + 8]
                sums[row] = term if sums[row] is None else sums[row] + term
    stacked = jnp.concatenate(sums, axis=0).astype(BF16)
    out_row = iota((2 * ROWS, 2 * ROWS), 0)
    in_row = iota((2 * ROWS, 2 * ROWS), 1)
    packed = lax.rem(out_row, ROWS)
    from_row = 8 * (packed // SCORE) + SCORE * (out_row // ROWS) + lax.rem(packed, SCORE)
    sorted_rows = mm(hot(in_row == from_row), stacked).astype(BF16)
    left = jnp.concatenate([sorted_rows[0:ROWS], sorted_rows[ROWS : 2 * ROWS]], axis=1)
    mixs[...] = left
    for delta in (2, 1, 3):
        send(mixs, mixr.at[delta - 1], m_ss.at[delta - 1], m_rs.at[delta - 1], at_x(delta))
    own_weight.wait()
    product = mm(left, wown[...])
    landed(
        wx.at[:, pl.ds(pl.multiple_of(ROWS * (1 - core), ROWS), ROWS)],
        wy_ss.at[Y],
        wy_rs.at[Y],
        {"grp": 2 * level + 1 - core, "seg": me},
    )
    for delta in (1, 3, 2):
        landed(mixr.at[delta - 1], m_ss.at[delta - 1], m_rs.at[delta - 1], at_x(delta))
        product = product + mm(mixr[delta - 1], wx[delta - 1])
    zown[...] = product

    for delta in (4, 3, 5, 2, 6, 1, 7):
        target = lax.rem(z + delta, Z)
        zsend[delta] = encode(zown[pl.ds(pl.multiple_of(16 * target, 16), 16), :])
        send(zsend.at[delta], zrecv.at[delta], z_ss.at[delta], z_rs.at[delta], at_z(delta))
    hidden = zown[pl.ds(pl.multiple_of(16 * z, 16), 16), :] + rsend[0].astype(F32)
    for delta in range(1, X):
        landed(rrecv.at[delta - 1], r_ss.at[delta], r_rs.at[delta], at_x(delta))
        hidden = hidden + rrecv[delta - 1].astype(F32)
    for delta in (7, 1, 6, 2, 5, 3, 4):
        landed(zrecv.at[delta], z_ss.at[delta], z_rs.at[delta], at_z(delta))
        hidden = hidden + decode(zrecv[delta])
    squares = jnp.sum(hidden * hidden, axis=1, keepdims=True)
    sqs[...] = jnp.broadcast_to(squares, sqs.shape)
    for delta in (2, 1, 3):
        send(sqs, sqr.at[delta - 1], s_ss.at[delta - 1], s_rs.at[delta - 1], at_x(delta))
    gain = gain_ref[dx_cols(x)].astype(F32).reshape(1, DX)
    for delta in (1, 3, 2):
        landed(sqr.at[delta - 1], s_ss.at[delta - 1], s_rs.at[delta - 1], at_x(delta))
    power = (sqs[...] + sqr[0] + sqr[1] + sqr[2])[:, 0:1] / D
    normed = (hidden * lax.rsqrt(power + 1e-06) * gain).astype(BF16)

    def drain():
        for copy in pending:
            copy.wait_send()
        for target, copy in guarded:

            @pl.when(target != z)
            def _():
                copy.wait_send()

    return normed, drain


def front_scratch():
    sems = pltpu.SemaphoreType.DMA
    return [
        pltpu.VMEM((SLOTS, 2 * ROWS, HEAD), BF16),
        pltpu.VMEM((KV_HEADS, TOK, 2 * ROWS), F32),
        pltpu.VMEM((2, 2 * WINDOW - 1, 8, 2 * ROWS), F32),
        pltpu.VMEM((2, 8, 2 * ROWS), F32),
        pltpu.VMEM((KV_HEADS, X, 8 * WINDOW, HEAD), F32),
        pltpu.VMEM((KV_HEADS, X - 1, 8 * WINDOW, HEAD), F32),
        pltpu.VMEM((KV_HEADS, 8 * OWNERS, HEAD), F32),
        pltpu.VMEM((Z, 8 * OWNERS, HEAD), F32),
        pltpu.VMEM((ROWS, 2 * HEAD), BF16),
        pltpu.VMEM((X - 1, ROWS, 2 * HEAD), BF16),
        pltpu.VMEM((2 * HEAD, DX), BF16),
        pltpu.VMEM((X - 1, 2 * HEAD, DX), BF16),
        pltpu.VMEM((X, 16, DX), BF16),
        pltpu.VMEM((X - 1, 16, DX), BF16),
        pltpu.VMEM((Z, 16, DX + HEAD), jnp.int16),
        pltpu.VMEM((ROWS, DX), F32),
        pltpu.VMEM((Z, 16, DX + HEAD), jnp.int16),
        pltpu.VMEM((16, HEAD), F32),
        pltpu.VMEM((X - 1, 16, HEAD), F32),
        sems,
        sems((2, WINDOW)),
        sems((2, WINDOW)),
        sems((2, 2 * WINDOW - 1)),
        sems((2, 2 * WINDOW - 1)),
        sems((KV_HEADS, X - 1)),
        sems((KV_HEADS, X - 1)),
        sems((Z,)),
        sems((Z,)),
        sems((X - 1,)),
        sems((X - 1,)),
        sems((X - 1,)),
        sems((X - 1,)),
        sems((GRP,)),
        sems((GRP,)),
        sems((X,)),
        sems((X,)),
        sems((Z,)),
        sems((Z,)),
        sems((X - 1,)),
        sems((X - 1,)),
    ]


def encode(value):
    most = jnp.maximum(jnp.max(jnp.abs(value), axis=1, keepdims=True), 1e-30)
    level = jnp.ceil(jnp.log2(most * (1.0 / 32000.0)))
    scaled = jnp.round(value * jnp.exp2(-level)).astype(jnp.int32)
    levels = jnp.broadcast_to(level.astype(jnp.int32), (value.shape[0], HEAD))
    return jnp.concatenate([scaled, levels], axis=1).astype(jnp.int16)


def decode(code):
    wide = code.astype(jnp.int32).astype(F32)
    return wide[:, 0:DX] * jnp.exp2(wide[:, DX : DX + 1])


def vmem():
    return pl.BlockSpec(memory_space=pltpu.VMEM)


SIZE = {"x": X, "y": Y, "z": Z}
DIRECT = "xy"


def plan_gather():
    messages = []
    by_key = {}
    for part, (offset, width, order) in enumerate(PARTS):
        for stage, axis in enumerate(order):
            count = SIZE[axis]
            chunked = stage == 2
            inner = range(SIZE[order[1]]) if chunked else (None,)
            amount = 32 * width
            for name in order[:stage]:
                amount *= SIZE[name]
            if chunked:
                amount //= SIZE[order[1]]
            if stage == 0 and axis in DIRECT:
                for step in range(1, count):
                    by_key[part, stage, step, None, 1] = len(messages)
                    messages.append(
                        dict(
                            part=part, stage=stage, axis=axis, step=step, chunk=None, way=1, half=None,
                            size=amount, hops=min(step, count - step), link=1 if 2 * step <= count else -1, direct=True,
                        )
                    )
                continue
            for step in range(1, count // 2 + 1):
                for rank, chunk in enumerate(inner):
                    for way in (1, -1):
                        half = None
                        if step == count // 2:
                            if chunked:
                                if (way > 0) != (rank % 2 == 0):
                                    continue
                            elif stage == 0:
                                if way < 0:
                                    continue
                            else:
                                half = 0 if way > 0 else 1
                        key = (part, stage, step, chunk, way)
                        by_key[key] = len(messages)
                        messages.append(
                            dict(
                                part=part, stage=stage, axis=axis, step=step, chunk=chunk, way=way, half=half,
                                size=amount if half is None else amount // 2, hops=1, link=way, direct=False,
                            )
                        )

    def bringing(part, stage, offset):
        count = SIZE[PARTS[part][2][stage]]
        offset %= count
        if offset == 0:
            return []
        found = []
        for key, index in by_key.items():
            if key[0] == part and key[1] == stage and (-key[4] * key[2]) % count == offset:
                found.append(index)
        return found

    def whole_stage(part, stage):
        return [index for key, index in by_key.items() if key[0] == part and key[1] == stage]

    for message in messages:
        part, stage = message["part"], message["stage"]
        if message["step"] > 1 and not message["direct"]:
            if message["chunk"] is None:
                needs = bringing(part, stage, -message["way"] * (message["step"] - 1))
            else:
                needs = [by_key[part, stage, message["step"] - 1, message["chunk"], message["way"]]]
        elif stage == 0:
            needs = []
        elif stage == 1:
            needs = whole_stage(part, 0)
        elif message["chunk"] == 0:
            needs = whole_stage(part, 0)
        else:
            needs = bringing(part, 1, message["chunk"])
        message["needs"] = needs
    tasks = []
    for part, (offset, width, order) in enumerate(PARTS):
        count = SIZE[order[2]]
        groups = [(0,)] + [(step, -step) for step in range(1, count // 2)] + [(count // 2,)]
        if part == 1:
            groups = [(item,) for group in groups for item in group]
        for group in groups:
            needs = []
            for item in group:
                if item == 0:
                    needs += whole_stage(part, 0) + whole_stage(part, 1)
                else:
                    needs += bringing(part, 2, item)
            tasks.append(dict(part=part, group=group, needs=needs))

    free = {}
    ready = {}
    arrive = {}
    left = set(range(len(messages)))
    while left:
        best = None
        for index in sorted(left):
            message = messages[index]
            if all(need in arrive for need in message["needs"]):
                at = max([arrive[need] for need in message["needs"]], default=0.0)
                link = (message["axis"], message["link"])
                begin = max(at, free.get(link, 0.0))
                if best is None or (begin, at, index) < best[0]:
                    best = ((begin, at, index), index, link, at)
        (begin, at, unused), index, link, at = best
        left.remove(index)
        finish = begin + messages[index]["hops"] * messages[index]["size"] / 46e3
        free[link] = finish
        ready[index] = at
        arrive[index] = finish + 0.9
    events = [(ready[index], 0, index) for index in ready]
    events += [
        (max(arrive[need] for need in task["needs"]) + 0.2, 1, number) for number, task in enumerate(tasks)
    ]
    return messages, tasks, sorted(events)


GATHERS = len(plan_gather()[0])


def merge_tiles(tiles):
    peak = tiles[0]
    for tile in tiles[1:]:
        peak = jnp.maximum(peak, tile)
    raised = jnp.exp(tiles[0] - peak)
    added = tiles[0]
    for tile in tiles[1:]:
        raised = raised + jnp.exp(tile - peak)
        added = added + tile
    return jnp.where(iota(peak.shape, 0) == 0, peak + jnp.log(raised), added)


def program_body(
    q_hbm, k_hbm, v_hbm, node_hbm, par_hbm, pos_hbm, ow_hbm, resid_hbm, gain_ref,
    w_hbm, leaf_hbm, target_hbm, old_hbm, adv_hbm,
    answer_ref,
    q_ref, k_ref, v_ref, node_ref, par_ref, pos_ref, resid_ref, leaf_ref, target_ref, old_ref, adv_ref,
    in_sems, *rest,
):
    front_count = len(front_scratch())
    front_refs = rest[:front_count]
    (
        w, part_a, part_b, part_c, logits, paths, tiny, info, info_x, info_z, info_y,
        stat_s, stat_y, stat_z, mine_x, last_s, last_r,
        w_sem, w_ss, w_rs, g_ss, g_rs, i_ss, i_rs, t_ss, t_rs, y_ss, y_rs, l_ss, l_rs,
    ) = rest[front_count:]
    grp = lax.axis_index("grp")
    me = lax.axis_index("seg")
    y = grp // 2
    core = lax.rem(grp, 2)
    z = me // X
    x = lax.rem(me, X)
    at = {"x": x, "y": y, "z": z}
    size = {"x": X, "y": Y, "z": Z}

    def peer(axis, delta):
        moved = dict(at)
        moved[axis] = lax.rem(at[axis] + delta + size[axis], size[axis])
        return {"grp": moved["y"] * 2 + core, "seg": moved["z"] * X + moved["x"]}

    barrier = pltpu.get_barrier_semaphore()
    offsets = [way * delta for delta in range(1, WINDOW) for way in (1, -1)]
    offsets += [delta for delta in range(X, SEG, X) if min(delta, SEG - delta) >= WINDOW]
    partners = [{"seg": lax.rem(me + delta + SEG, SEG)} for delta in offsets]
    partners += [{"grp": lax.rem(grp + delta, GRP), "seg": me} for delta in range(1, GRP)]
    partners += [
        {"grp": lax.rem(y + dy, Y) * 2 + core, "seg": z * X + lax.rem(x + dx, X)}
        for dy in range(1, Y)
        for dx in range(1, X)
    ]
    for partner in partners:
        pl.semaphore_signal(barrier, 1, device_id=partner)
    loads = []
    for index, (src, dst) in enumerate(
        (
            (q_hbm, q_ref), (k_hbm, k_ref), (v_hbm, v_ref), (node_hbm, node_ref), (par_hbm, par_ref),
            (pos_hbm, pos_ref), (resid_hbm, resid_ref), (leaf_hbm, leaf_ref),
            (target_hbm, target_ref), (old_hbm, old_ref), (adv_hbm, adv_ref),
        )
    ):
        copy = pltpu.make_async_copy(src, dst, in_sems.at[index])
        copy.start()
        loads.append(copy)
    own_w = pltpu.make_async_copy(w_hbm, w.at[:, 0:VOC], w_sem)
    loads[0].wait()

    tile_sub = iota((8, ROWS), 0)
    tile_lane = iota((8, ROWS), 1)
    pending = []
    swap = pltpu.make_async_remote_copy(
        src_ref=w_hbm,
        dst_ref=w.at[:, VOC : 2 * VOC],
        send_sem=w_ss,
        recv_sem=w_rs,
        device_id={"grp": y * 2 + 1 - core, "seg": me},
    )

    def spread(axis, sources, into, base, ss, rs):
        count = size[axis]
        here = at[axis]
        for delta in range(1, count):
            there = lax.rem(here + delta, count)
            copy = pltpu.make_async_remote_copy(
                src_ref=sources(there),
                dst_ref=into.at[here],
                send_sem=ss.at[base + delta],
                recv_sem=rs.at[base + here],
                device_id=peer(axis, delta),
            )
            copy.start()
            pending.append(copy)

    def collect(axis, into, base, ss, rs):
        count = size[axis]
        here = at[axis]
        for delta in range(1, count):
            there = lax.rem(here + delta, count)
            pltpu.make_async_remote_copy(
                src_ref=into.at[there],
                dst_ref=into.at[there],
                send_sem=ss.at[base + delta],
                recv_sem=rs.at[base + there],
                device_id=peer(axis, delta),
            ).wait_recv()

    bufs = (part_a, part_b, part_c)
    messages, tasks, events = plan_gather()

    def block(message, moved):
        axis, stage = message["axis"], message["stage"]
        order = PARTS[message["part"]][2]
        where = []
        for name in "xyz":
            if name == axis:
                where.append(lax.rem(at[name] + moved + 2 * size[name], size[name]))
            elif name not in order[:stage]:
                where.append(at[name])
            elif message["chunk"] is not None and name == order[1]:
                where.append(lax.rem(at[name] + message["chunk"], size[name]))
            elif message["half"] is not None and name == order[0]:
                cut = size[name] // 2
                where.append(pl.ds(message["half"] * cut, cut))
            else:
                where.append(slice(None))
        return bufs[message["part"]].at[tuple(where)]

    def ring(index, moved):
        message = messages[index]
        ref = block(message, moved)
        return pltpu.make_async_remote_copy(
            src_ref=ref,
            dst_ref=ref,
            send_sem=g_ss.at[index],
            recv_sem=g_rs.at[index],
            device_id=peer(message["axis"], message["step"] if message["direct"] else message["way"]),
        )

    def head_task(task):
        part = task["part"]
        offset, width, order = PARTS[part]
        buf = bufs[part]
        axis = order[2]

        def columns(n, carry):
            cols = pl.ds(pl.multiple_of(256 * n, 256), 256)
            if axis == "x":
                here = lax.rem(x + task["group"][0] + X, X)
                rows = buf[here].reshape(Y * Z * 16, width)
                weight = w[pl.ds(pl.multiple_of(DX * here + offset, 128), width), cols]
                logits[:, :, :, cols] = logits[:, :, :, cols] + mm(rows, weight).reshape(Y, Z, 16, 256)
                return carry
            places = [lax.rem(at[axis] + item + size[axis], size[axis]) for item in task["group"]]
            total = None
            for index in range(X):
                if axis == "z":
                    rows = [buf[index, :, place].reshape(Y * 16, width) for place in places]
                else:
                    rows = [buf[index, place].reshape(Z * 16, width) for place in places]
                rows = rows[0] if len(rows) == 1 else jnp.concatenate(rows, axis=0)
                term = mm(rows, w[DX * index + offset : DX * index + offset + width, cols])
                total = term if total is None else total + term
            high = total.shape[0] // len(places)
            for number, place in enumerate(places):
                piece = total[high * number : high * number + high]
                if axis == "z":
                    logits[:, place, :, cols] = logits[:, place, :, cols] + piece.reshape(Y, 16, 256)
                else:
                    logits[place, :, :, cols] = logits[place, :, :, cols] + piece.reshape(Z, 16, 256)
            return carry

        lax.fori_loop(0, 2 * VOC // 256, columns, 0)

    def tell():
        tiny[...] = jnp.zeros_like(tiny)
        tiny[0:1, 0:SCORE] = target_ref[...].astype(F32)
        tiny[1:2, 0:SCORE] = old_ref[...]
        tiny[2:3, 0:2] = adv_ref[...]
        start = tiny[...]
        info[...] = jnp.where(
            tile_sub < 2, pltpu.roll(start, SCORE * me, 1), pltpu.roll(start, 2 * me, 1)
        )
        info_x[x] = info[...]
        spread("x", lambda there: info_x.at[x], info_x, 0, i_ss, i_rs)
        yield
        collect("x", info_x, 0, i_ss, i_rs)
        info_z[z] = info_x[0] + info_x[1] + info_x[2] + info_x[3]
        spread("z", lambda there: info_z.at[z], info_z, X, i_ss, i_rs)
        yield
        collect("z", info_z, X, i_ss, i_rs)
        whole = info_z[0]
        for index in range(1, Z):
            whole = whole + info_z[index]
        info_y[y] = whole
        spread("y", lambda there: info_y.at[y], info_y, X + Z, i_ss, i_rs)
        yield
        collect("y", info_y, X + Z, i_ss, i_rs)

    talk = tell()

    def greet():
        pl.semaphore_wait(barrier, len(partners))

    def early():
        own_w.start()
        swap.start()
        for copy in loads[1:]:
            copy.wait()
        next(talk)

    def middle(closure_t, row_hot_t):
        next(talk)
        logits[...] = jnp.zeros_like(logits)
        leaf_hot_t = hot(iota((NODES, LEAVES), 0) == leaf_ref[...])
        leaf_reach_t = mm(closure_t, leaf_hot_t)
        filler = jnp.zeros((NODES, NODES - LEAVES), F32)
        leaf_reach = jnp.concatenate([leaf_reach_t, filler], axis=1).T
        paths[...] = mm(leaf_reach.astype(BF16), row_hot_t)

    normed, drain = front(
        me, grp, q_ref, k_ref, v_ref, node_ref, par_ref, pos_ref, ow_hbm, resid_ref, gain_ref,
        *front_refs, greet, early, middle,
    )
    for (offset, width, order), buf in zip(PARTS, bufs):
        buf[x, y, z] = normed[:, offset : offset + width]
    next(talk)
    seen = set()

    def await_all(needs):
        for index in needs:
            if index not in seen:
                seen.add(index)
                ring(index, -messages[index]["way"] * messages[index]["step"]).wait_recv()

    loaded = False
    for unused, kind, index in events:
        if kind == 0:
            await_all(messages[index]["needs"])
            back = 0 if messages[index]["direct"] else messages[index]["step"] - 1
            copy = ring(index, -messages[index]["way"] * back)
            copy.start()
            pending.append(copy)
        else:
            if not loaded:
                own_w.wait()
                swap.wait_recv()
                loaded = True
            await_all(tasks[index]["needs"])
            head_task(tasks[index])
    for rest_of in talk:
        pass

    voc_lane = iota((ROWS, 2 * VOC), 1)
    own_base = (grp * SEG + me) * VOC
    other_base = ((2 * y + 1 - core) * SEG + me) * VOC - VOC
    voc_id = (voc_lane + jnp.where(voc_lane < VOC, own_base, other_base)).astype(F32)
    targets = jnp.concatenate(
        [info_y[...].reshape(8 * Y, ROWS), jnp.zeros((ROWS - 8 * Y, ROWS), F32)], axis=0
    ).T
    square_lane = iota((ROWS, ROWS), 1)
    for index in range(Y):
        block = logits[index].reshape(ROWS, 2 * VOC)
        top = jnp.max(block, axis=1, keepdims=True)
        lse = top + jnp.log(jnp.sum(jnp.exp(block - top), axis=1, keepdims=True))
        found = voc_id == targets[:, 8 * index : 8 * index + 1]
        picked = jnp.sum(jnp.where(found, block, 0.0), axis=1, keepdims=True)
        both = jnp.where(square_lane == 0, lse, jnp.where(square_lane == 1, picked, 0.0))
        stat_s[index] = both.T[0:8]
    def square(dy, dx):
        ty = lax.rem(y + dy, Y)
        tx = lax.rem(x + dx, X)
        device = {"grp": ty * 2 + core, "seg": z * X + tx}
        return ty, tx, device

    steps = [(dy, dx) for dy in range(Y) for dx in range(X) if dy or dx]
    for dy, dx in steps:
        ty, tx, device = square(dy, dx)
        copy = pltpu.make_async_remote_copy(
            src_ref=stat_s.at[ty],
            dst_ref=stat_y.at[y * X + x],
            send_sem=y_ss.at[dy * X + dx],
            recv_sem=y_rs.at[y * X + x],
            device_id=device,
        )
        copy.start()
        pending.append(copy)
    stat_y[y * X + x] = stat_s[y]

    path = paths[...]
    counts = jnp.maximum(jnp.sum(path, axis=1, keepdims=True), 1.0)
    for dy, dx in steps:
        ty, tx, device = square(dy, dx)
        pltpu.make_async_remote_copy(
            src_ref=stat_s.at[ty],
            dst_ref=stat_y.at[ty * X + tx],
            send_sem=y_ss.at[dy * X + dx],
            recv_sem=y_rs.at[ty * X + tx],
            device_id=device,
        ).wait_recv()
    mine_x[...] = merge_tiles([stat_y[index] for index in range(X * Y)])
    spread("z", lambda there: mine_x, stat_z, Y + X, t_ss, t_rs)
    stat_z[z] = mine_x[...]
    collect("z", stat_z, Y + X, t_ss, t_rs)
    merged = merge_tiles([stat_z[index] for index in range(Z)])

    own_info = info_y[y]
    token_row = merged[1:2] - merged[0:1] - own_info[1:2]
    shift = lax.rem(ROWS - SCORE * me, ROWS)
    answer_ref[0:1, :] = pltpu.roll(jnp.broadcast_to(token_row, (8, ROWS)), shift, 1)[0:1]
    means = jnp.sum(path * token_row, axis=1, keepdims=True) / counts
    leaf_row = jnp.broadcast_to(means, (ROWS, ROWS)).T[0:8]
    answer_ref[1:2, :] = pltpu.roll(leaf_row, lax.rem(ROWS - 2 * me, ROWS), 1)[0:1]
    gains = own_info[2:3]
    ratio = jnp.exp(leaf_row)
    terms = jnp.minimum(ratio * gains, jnp.clip(ratio, 1.0 - EPS_LOW, 1.0 + EPS_HIGH) * gains)
    terms = jnp.where((tile_sub == 0) & (tile_lane < LEAVES), terms, 0.0)
    last_s[...] = terms

    last = []
    for delta in range(1, GRP):
        copy = pltpu.make_async_remote_copy(
            src_ref=last_s,
            dst_ref=last_r.at[grp],
            send_sem=l_ss.at[delta],
            recv_sem=l_rs.at[grp],
            device_id={"grp": lax.rem(grp + delta, GRP), "seg": me},
        )
        copy.start()
        last.append(copy)
    last_r[grp] = terms
    for delta in range(1, GRP):
        there = lax.rem(grp + delta, GRP)
        pltpu.make_async_remote_copy(
            src_ref=last_s,
            dst_ref=last_r.at[there],
            send_sem=l_ss.at[delta],
            recv_sem=l_rs.at[there],
            device_id={"grp": there, "seg": me},
        ).wait_recv()
    everything = last_r[0]
    for index in range(1, GRP):
        everything = everything + last_r[index]
    total = -jnp.sum(everything, axis=(0, 1), keepdims=True) / (LEAVES * GRP)
    answer_ref[2:8, :] = jnp.broadcast_to(total, (6, ROWS))

    drain()
    for copy in pending:
        copy.wait_send()
    swap.wait_send()
    for copy in last:
        copy.wait_send()


def split_body(answer_ref, token_ref, leaf_ref, loss_ref):
    token_ref[...] = answer_ref[0:1, 0:SCORE]
    leaf_ref[...] = answer_ref[1:2, 0:2]
    loss_ref[...] = answer_ref[2:3, 0:1]


def body(
    queries, keys, values, node_ids, parents, score_pos, out_weight, resid, norm_gain,
    vocab_weight, targets, old_logp, leaf_node, advantages,
):
    sems = pltpu.SemaphoreType.DMA
    tile = pltpu.VMEM((8, ROWS), F32)

    def tiles(count):
        return pltpu.VMEM((count, 8, ROWS), F32)

    anywhere = pl.BlockSpec(memory_space=pl.ANY)
    answer = pl.pallas_call(
        program_body,
        out_shape=jax.ShapeDtypeStruct((8, ROWS), F32),
        in_specs=[anywhere] * 8 + [vmem()] + [anywhere] * 5,
        out_specs=vmem(),
        scratch_shapes=[
            pltpu.VMEM((SCORE, 64 * HEAD), BF16),
            pltpu.VMEM((TOK, KV_HEADS * HEAD), BF16),
            pltpu.VMEM((TOK, KV_HEADS * HEAD), BF16),
            pltpu.VMEM((SEG, TOK), jnp.int32),
            pltpu.VMEM((1, NODES), jnp.int32),
            pltpu.VMEM((1, ROWS), jnp.int32),
            pltpu.VMEM((SCORE, D), BF16),
            pltpu.VMEM((1, LEAVES), jnp.int32),
            pltpu.VMEM((1, SCORE), jnp.int32),
            pltpu.VMEM((1, SCORE), F32),
            pltpu.VMEM((1, 2), F32),
            sems((11,)),
        ]
        + front_scratch()
        + [pltpu.VMEM((D, 2 * VOC), BF16)]
        + [pltpu.VMEM((X, Y, Z, 16, width), BF16) for offset, width, order in PARTS]
        + [
            pltpu.VMEM((Y, Z, 16, 2 * VOC), F32),
            pltpu.VMEM((NODES, ROWS), F32),
            tile,
            tile,
            tiles(X),
            tiles(Z),
            tiles(Y),
            tiles(Y),
            tiles(X * Y),
            tiles(Z),
            tile,
            tile,
            tiles(GRP),
            sems,
            sems,
            sems,
            sems((GATHERS,)),
            sems((GATHERS,)),
            sems((X + Y + Z,)),
            sems((X + Y + Z,)),
            sems((X + Y + Z,)),
            sems((X + Y + Z,)),
            sems((X * Y,)),
            sems((X * Y,)),
            sems((GRP,)),
            sems((GRP,)),
        ],
        compiler_params=pltpu.CompilerParams(
            collective_id=0, has_side_effects=True, vmem_limit_bytes=58 * MIB
        ),
    )(
        queries[0], keys[0], values[0], node_ids.reshape(SEG, TOK), parents, score_pos, out_weight,
        resid[0], norm_gain, vocab_weight, leaf_node, targets, old_logp, advantages,
    )
    token, leaf, loss = pl.pallas_call(
        split_body,
        out_shape=(
            jax.ShapeDtypeStruct((1, SCORE), F32),
            jax.ShapeDtypeStruct((1, 2), F32),
            jax.ShapeDtypeStruct((1, 1), F32),
        ),
        in_specs=[vmem()],
        out_specs=(vmem(), vmem(), vmem()),
    )(answer)
    return (token, leaf, loss.reshape(()))


def solution(mesh):
    placed = (
        P("grp", "seg", None),
        P("grp", "seg", None),
        P("grp", "seg", None),
        P("grp", None),
        P("grp", None),
        P("grp", None),
        P("seg", None),
        P("grp", "seg", None),
        P(),
        P(None, ("grp", "seg")),
        P("grp", "seg"),
        P("grp", "seg"),
        P("grp", None),
        P("grp", "seg"),
    )
    return jax.shard_map(
        body,
        mesh=mesh,
        in_specs=placed,
        out_specs=(P("grp", "seg"), P("grp", "seg"), P()),
        check_vma=False,
    )
```
